32 devices in a mesh: groups: 2 (over y), ctx: 4 (over x, core), tp: 4 (over z).
Axes of the slice: x: 2, y: 2, z: 4, core: 2. Of those that a mesh axis runs over, the one named last changes fastest.
Arguments:
- tokens: bfloat16 [2048, 4096], P(('groups', 'ctx', 'tp')), parts along dimension 0, may hold values from -6 to 6
- gate_weight: bfloat16 [4096, 8192], P(None, 'tp'), may hold values from -0.09375 to 0.09375
- value_weight: bfloat16 [4096, 8192], P(None, 'tp'), may hold values from -0.09375 to 0.09375
- key_weight: bfloat16 [4096, 1024], P(None, 'tp'), may hold values from -0.09375 to 0.09375
- query_weight: bfloat16 [4096, 1024], P(None, 'tp'), may hold values from -0.09375 to 0.09375
- step_weight: bfloat16 [4096, 128], P(None, 'tp'), may hold values from -0.09375 to 0.09375
- value_conv: float32 [4, 8192], P(None, 'tp'), may hold values from -3 to 3
- key_conv: float32 [4, 1024], P(None, 'tp'), may hold values from -3 to 3
- query_conv: float32 [4, 1024], P(None, 'tp'), may hold values from -3 to 3
- step_bias: float32 [128], P('tp'), may hold values from -3 to -1
- decay_log: float32 [128], P('tp'), may hold values from -6.5 to -1.5
- skip_gain: float32 [128], P('tp'), may hold values from 0.5 to 1.5
- norm_gain: float32 [8192], P('tp'), may hold values from 0.1 to 1.9
- out_weight: bfloat16 [8192, 4096], P('tp'), may hold values from -0.0625 to 0.0625
Outputs:
- layer_out: bfloat16 [2048, 4096], P(('groups', 'ctx', 'tp')), parts along dimension 0
The draws below stay inside these ranges and needn't reach their ends.
There are 2 independent parts, one for each index of `groups`. The reference program is written for one: setup_inputs(seed, part) draws one part's arguments, and reference() takes and returns one part's arrays. A program takes and returns all parts, laid end to end along the dimension named above; an argument that names none is the same for every part. Nothing has to cross between parts.
All inputs are finite; a program needn't handle non-finite values.
Results may differ from the reference program's by a relative error of at most 0.024.
Values may be sent and summed in bfloat16 or wider, within the bound.
A program may use at most 192 MiB of HBM per device.

```python
import jax
import jax.numpy as jnp
from jax import lax

D = 4096
HEADS = 128
HEAD_DIM = 64
STATE = 128
GROUPS = 8
CONV = 4
INNER = 8192
BLOCK = 128
SEQ = 1024
N_TP = 4


def block_levels(key, shape, cuts, least, top_value):
    def one(dim, parts):
        draws = jax.random.uniform(jax.random.fold_in(jax.random.fold_in(key, 6), dim), (parts,), jnp.float32, least / len(cuts), top_value / len(cuts))
        return jnp.repeat(jnp.exp(draws), shape[dim] // parts).reshape((-1,) + (1,) * (len(shape) - dim - 1))

    gain = one(*cuts[0])
    for cut in cuts[1:]:
        gain = gain * one(*cut)
    return gain


def normal_values(stream_key, extent, spread, most, shards=(), held_as=jnp.bfloat16):
    loudness = block_levels(stream_key, extent, shards, -0.22, 0.18) if shards else 1.0
    entries = jax.random.normal(stream_key, extent, jnp.float32) * spread * loudness
    return jnp.minimum(jnp.maximum(entries, -most), most).astype(held_as)


def setup_inputs(seed: int = 0, part: int = 0) -> dict:
    streams_of = jax.random.split(jax.random.key(seed), 15)
    own_keys = jax.random.split(jax.random.fold_in(streams_of[14], part), 15)
    return {
        "tokens": normal_values(own_keys[0], (SEQ, D), 1.0, 6.0, ((0, 16),)),
        "gate_weight": normal_values(streams_of[1], (D, INNER), D ** -0.5, 0.09375, ((1, 4),)),
        "value_weight": normal_values(streams_of[2], (D, INNER), D ** -0.5, 0.09375, ((1, 4),)),
        "key_weight": normal_values(streams_of[3], (D, GROUPS * STATE), D ** -0.5, 0.09375, ((1, 4),)),
        "query_weight": normal_values(streams_of[4], (D, GROUPS * STATE), D ** -0.5, 0.09375, ((1, 4),)),
        "step_weight": normal_values(streams_of[5], (D, HEADS), D ** -0.5, 0.09375, ((1, 4),)),
        "value_conv": normal_values(streams_of[6], (CONV, INNER), CONV ** -0.5, 3.0, ((1, 4),), jnp.float32),
        "key_conv": normal_values(streams_of[7], (CONV, GROUPS * STATE), CONV ** -0.5, 3.0, ((1, 4),), jnp.float32),
        "query_conv": normal_values(streams_of[8], (CONV, GROUPS * STATE), CONV ** -0.5, 3.0, ((1, 4),), jnp.float32),
        "step_bias": jnp.clip(-3.0 + 2.0 * jax.random.uniform(streams_of[9], (HEADS,), jnp.float32) ** block_levels(streams_of[9], (HEADS,), ((0, 4),), -0.2, 0.2), -3.0, -1.0),
        "decay_log": jnp.clip(-6.5 + 5.0 * jax.random.uniform(streams_of[10], (HEADS,), jnp.float32) ** block_levels(streams_of[10], (HEADS,), ((0, 4),), -0.2, 0.2), -6.5, -1.5),
        "skip_gain": jnp.clip(0.5 + 1.0 * jax.random.uniform(streams_of[11], (HEADS,), jnp.float32) ** block_levels(streams_of[11], (HEADS,), ((0, 4),), -0.2, 0.2), 0.5, 1.5),
        "norm_gain": jnp.clip(1.0 + 0.18 * jax.random.normal(streams_of[12], (INNER,), jnp.float32), 0.1, 1.9),
        "out_weight": normal_values(streams_of[13], (INNER, D), INNER ** -0.5, 0.0625, ((0, 4),)),
    }


def causal_mix(padded, kernel, length):
    total = padded[0:length] * kernel[0]
    for tap_index in range(1, kernel.shape[0]):
        total = total + padded[tap_index:tap_index + length] * kernel[tap_index]
    return total

def convolve(pre, kernel):
    padded = jnp.pad(pre.astype(jnp.float32), ((CONV - 1, 0), (0, 0)))
    return jax.nn.silu(causal_mix(padded, kernel, SEQ)).astype(jnp.bfloat16)

def reference(tokens, gate_weight, value_weight, key_weight, query_weight, step_weight, value_conv, key_conv, query_conv, step_bias, decay_log, skip_gain, norm_gain, out_weight):
    gate_in = jnp.dot(tokens, gate_weight, preferred_element_type=jnp.float32).astype(jnp.bfloat16)
    value_pre = jnp.dot(tokens, value_weight, preferred_element_type=jnp.float32).astype(jnp.bfloat16)
    key_pre = jnp.dot(tokens, key_weight, preferred_element_type=jnp.float32).astype(jnp.bfloat16)
    query_pre = jnp.dot(tokens, query_weight, preferred_element_type=jnp.float32).astype(jnp.bfloat16)
    step_raw = jnp.dot(tokens, step_weight, preferred_element_type=jnp.float32)
    value_act = convolve(value_pre, value_conv)
    key_act = convolve(key_pre, key_conv)
    query_act = convolve(query_pre, query_conv)
    step = jax.nn.softplus(step_raw + step_bias)
    rate = -jnp.exp(decay_log) * step
    block_count = SEQ // BLOCK
    per_group = HEADS // GROUPS
    cum = jnp.cumsum(rate.reshape(block_count, BLOCK, HEADS), axis=1)
    steps_blk = step.reshape(block_count, BLOCK, HEADS)
    values = value_act.reshape(block_count, BLOCK, HEADS, HEAD_DIM)
    keys = key_act.reshape(block_count, BLOCK, GROUPS, STATE)
    queries = query_act.reshape(block_count, BLOCK, GROUPS, STATE)
    causal = jnp.tril(jnp.ones((BLOCK, BLOCK), jnp.bool_))

    def one_block(carry, item):
        cum_b, step_b, value_b, key_b, query_b = item
        scores = jnp.einsum('tgn,ugn->gtu', query_b.astype(jnp.float32), key_b.astype(jnp.float32))
        scores = jnp.repeat(scores, per_group, axis=0)
        cum_t = cum_b.T
        diff = cum_t[:, :, None] - cum_t[:, None, :]
        factor = jnp.where(causal, jnp.exp(jnp.where(causal, diff, 0.0)), 0.0)
        weights = (scores * factor * step_b.T[:, None, :]).astype(jnp.bfloat16)
        inner = jnp.einsum('htu,uhp->thp', weights.astype(jnp.float32), value_b.astype(jnp.float32))
        tail = jnp.exp(cum_b[-1:] - cum_b) * step_b
        weighted = (value_b.astype(jnp.float32) * tail[:, :, None]).astype(jnp.bfloat16)
        key_heads = jnp.repeat(key_b, per_group, axis=1)
        query_heads = jnp.repeat(query_b, per_group, axis=1)
        outer = jnp.einsum('thn,hnp->thp', query_heads.astype(jnp.float32), carry, precision=lax.Precision.HIGHEST)
        result = inner + jnp.exp(cum_b)[:, :, None] * outer + skip_gain[:, None] * value_b.astype(jnp.float32)
        local = jnp.einsum('uhn,uhp->hnp', key_heads.astype(jnp.float32), weighted.astype(jnp.float32))
        carry = jnp.exp(cum_b[-1])[:, None, None] * carry + local
        return (carry, result)
    start = jnp.zeros((HEADS, STATE, HEAD_DIM), jnp.float32)
    _, results = lax.scan(one_block, start, (cum, steps_blk, values, keys, queries))
    ssm_out = results.reshape(SEQ, INNER)
    gated = ssm_out * jax.nn.silu(gate_in.astype(jnp.float32))
    span = INNER // GROUPS
    grouped = gated.reshape(SEQ, GROUPS, span)
    scale = lax.rsqrt(lax.optimization_barrier(jnp.mean(grouped * grouped, axis=2)) + 1e-05)
    normed = ((grouped * scale[:, :, None]).reshape(SEQ, INNER) * norm_gain).astype(jnp.bfloat16)
    block_width = INNER // N_TP

    def add_block(total, block_index):
        first = (block_index * block_width).astype(jnp.int32)
        cols = lax.dynamic_slice_in_dim(normed, first, block_width, 1)
        rows = lax.dynamic_slice_in_dim(out_weight, first, block_width, 0)
        part = jnp.dot(cols, rows, preferred_element_type=jnp.float32).astype(jnp.bfloat16)
        part = lax.optimization_barrier(part)
        return (total + part.astype(jnp.float32), None)
    summed, _ = lax.scan(add_block, jnp.zeros((SEQ, D), jnp.float32), jnp.arange(N_TP, dtype=jnp.int32))
    return summed.astype(jnp.bfloat16)
```

```python
import functools

import jax
import jax.numpy as jnp
from jax import lax
from jax.experimental import pallas as pl
from jax.experimental.pallas import tpu as pltpu
from jax.sharding import PartitionSpec as P

STATE = 128
GROUPS = 8
INNER = 8192


def passed_along(shard, axis, by):
    count = lax.axis_size(axis)
    pairs = [(i, i + by) for i in range(count) if 0 <= i + by < count]
    return lax.ppermute(shard, axis, pairs)


def from_partner(block, axis, distance):
    count = lax.axis_size(axis)
    route = []
    for low in range(count):
        high = low | 1 << distance
        if high != low and high < count:
            route += [(low, high), (high, low)]
    return lax.ppermute(block, axis, route)


def causal_mix(padded, kernel, length):
    total = padded[0:length] * kernel[0]
    for tap_index in range(1, kernel.shape[0]):
        total = total + padded[tap_index : tap_index + length] * kernel[tap_index]
    return total


def shards(
    tokens,
    gate_weight,
    value_weight,
    key_weight,
    query_weight,
    step_weight,
    value_conv,
    key_conv,
    query_conv,
    step_bias,
    decay_log,
    skip_gain,
    norm_gain,
    out_weight,
):
    tok_dev = tokens.shape[0]
    slab_rows = tok_dev * lax.axis_size("tp")
    columns = gate_weight.shape[1]
    key_cols = key_weight.shape[1]
    heads_here = step_weight.shape[1]
    head_width = columns // heads_here
    block_len = min(128, slab_rows)
    block_count = slab_rows // block_len
    kernel_len = value_conv.shape[0]
    joined = jnp.concatenate(
        [gate_weight, value_weight, key_weight, query_weight, step_weight], axis=1
    )
    projected = jnp.dot(
        lax.all_gather(tokens, "tp", axis=0, tiled=True), joined, preferred_element_type=jnp.float32
    )
    gate_in = projected[:, :columns].astype(jnp.bfloat16)
    mixed_pre = projected[:, columns : 2 * columns + 2 * key_cols].astype(jnp.bfloat16)
    step_raw = projected[:, 2 * columns + 2 * key_cols :]
    border = passed_along(mixed_pre[slab_rows - (kernel_len - 1) :], "ctx", 1)
    padded = jnp.concatenate([border, mixed_pre], axis=0).astype(jnp.float32)
    kernel = jnp.concatenate([value_conv, key_conv, query_conv], axis=1)
    activated = jax.nn.silu(causal_mix(padded, kernel, slab_rows)).astype(jnp.bfloat16)
    value_act = activated[:, :columns]
    key_act = activated[:, columns : columns + key_cols]
    query_act = activated[:, columns + key_cols :]
    group_cols = max(key_cols, STATE)
    reach = group_cols // key_cols
    key_group, query_group = (key_act, query_act)
    for bit_index in range(reach.bit_length() - 1):
        other_keys, other_queries = from_partner((key_group, query_group), "tp", bit_index)
        upper = lax.axis_index("tp") // (1 << bit_index) % 2 == 1
        key_group = jnp.where(
            upper,
            jnp.concatenate([other_keys, key_group], 1),
            jnp.concatenate([key_group, other_keys], 1),
        )
        query_group = jnp.where(
            upper,
            jnp.concatenate([other_queries, query_group], 1),
            jnp.concatenate([query_group, other_queries], 1),
        )
    local_groups = group_cols // STATE
    per_group = heads_here // local_groups
    step = jax.nn.softplus(step_raw + step_bias)
    rate = -jnp.exp(decay_log) * step
    cum = jnp.cumsum(rate.reshape(block_count, block_len, heads_here), axis=1)
    step_blk = step.reshape(block_count, block_len, heads_here)
    values = value_act.reshape(block_count, block_len, heads_here, head_width)
    keys = key_group.reshape(block_count, block_len, local_groups, STATE)
    queries = query_group.reshape(block_count, block_len, local_groups, STATE)
    scores = jnp.einsum("btgn,bugn->gbtu", queries, keys, preferred_element_type=jnp.float32)
    scores = jnp.repeat(scores, per_group, axis=0)
    cum_t = jnp.transpose(cum, (2, 0, 1))
    step_t = jnp.transpose(step_blk, (2, 0, 1))
    causal = jnp.tril(jnp.ones((block_len, block_len), jnp.bool_))
    diff = cum_t[:, :, :, None] - cum_t[:, :, None, :]
    factor = jnp.where(causal, jnp.exp(jnp.where(causal, diff, 0.0)), 0.0)
    weights = (scores * factor * step_t[:, :, None, :]).astype(jnp.bfloat16)
    inner = jnp.einsum("hbtu,buhp->bthp", weights, values, preferred_element_type=jnp.float32)
    tail = jnp.exp(cum[:, -1:, :] - cum) * step_blk
    weighted = (values * tail[:, :, :, None]).astype(jnp.bfloat16)
    key_heads = jnp.repeat(keys, per_group, axis=2)
    query_heads = jnp.repeat(queries, per_group, axis=2)
    local = jnp.einsum("buhn,buhp->bhnp", key_heads, weighted, preferred_element_type=jnp.float32)
    falloff = jnp.exp(cum[:, -1, :])

    def advance(carry, item):
        fade, added = item
        return (fade[:, None, None] * carry + added, carry)

    zero_state = jnp.zeros((heads_here, STATE, head_width), jnp.float32)
    slab_state, _ = lax.scan(advance, zero_state, (falloff, local))
    slab_fall = jnp.exp(jnp.sum(cum[:, -1, :], axis=0))
    inflow = zero_state
    for turn in range(lax.axis_size("ctx") - 1):
        inflow = passed_along(
            (slab_fall[:, None, None] * inflow + slab_state).astype(jnp.bfloat16), "ctx", 1
        ).astype(jnp.float32)
    _, starts = lax.scan(advance, inflow, (falloff, local))
    outer = jnp.einsum(
        "bthn,bhnp->bthp", query_heads.astype(jnp.float32), starts, precision=lax.Precision.HIGHEST
    )
    ssm_out = (
        inner
        + jnp.exp(cum)[:, :, :, None] * outer
        + skip_gain[:, None] * values.astype(jnp.float32)
    )
    ssm_out = ssm_out.reshape(slab_rows, columns)
    gated = ssm_out * jax.nn.silu(gate_in.astype(jnp.float32))
    span = INNER // GROUPS
    piece_len = min(columns, span)
    norm_here = columns // piece_len
    squares = jnp.sum((gated * gated).reshape(slab_rows, norm_here, piece_len), axis=2)
    norm_reach = span // piece_len
    for bit_index in range(norm_reach.bit_length() - 1):
        squares = squares + from_partner(squares, "tp", bit_index)
    scale = lax.rsqrt(squares / span + 1e-05)
    normed = (gated.reshape(slab_rows, norm_here, piece_len) * scale[:, :, None]).reshape(
        slab_rows, columns
    ) * norm_gain
    normed = normed.astype(jnp.bfloat16)
    return lax.psum_scatter(
        jnp.dot(normed, out_weight, preferred_element_type=jnp.float32).astype(jnp.bfloat16),
        "tp",
        scatter_dimension=0,
        tiled=True,
    )


TILE = 256
BLOCK = 128
MESH = pl.DeviceIdType.MESH
EXACT = lax.Precision.HIGHEST


def greet(neighbours):
    barrier = pltpu.get_barrier_semaphore()
    count = 0
    for axis, index, exists in neighbours:

        @pl.when(exists)
        def _():
            pl.semaphore_signal(barrier, inc=1, device_id={axis: index}, device_id_type=MESH)

        count = count + exists.astype(jnp.int32)
    pl.semaphore_wait(barrier, count)


def project_kernel(
    n, tiles, tokens, gate_w, value_w, key_w, query_w, step_w, pre, step_raw,
    rows, weights, step_buf, weight_sem, step_sem, send_left, send_right, recv_sem,
):
    me = lax.axis_index("tp")
    length = tokens.shape[0]
    step_copy = pltpu.make_async_copy(step_w, step_buf, step_sem)
    step_copy.start()
    tile = 0
    for source in (gate_w, value_w, key_w, query_w):
        for part in range(source.shape[1] // TILE):
            pltpu.make_async_copy(
                source.at[:, pl.ds(part * TILE, TILE)], weights.at[tile], weight_sem.at[tile]
            ).start()
            tile += 1
    rows[me] = tokens[...]
    greet([("tp", me - 1, me > 0), ("tp", me + 1, me < n - 1)])

    def rightward(chunk):
        return pltpu.make_async_remote_copy(
            src_ref=rows.at[chunk], dst_ref=rows.at[chunk],
            send_sem=send_right.at[chunk], recv_sem=recv_sem.at[chunk],
            device_id={"tp": me + 1}, device_id_type=MESH,
        )

    def leftward(chunk):
        return pltpu.make_async_remote_copy(
            src_ref=rows.at[chunk], dst_ref=rows.at[chunk],
            send_sem=send_left.at[chunk], recv_sem=recv_sem.at[chunk],
            device_id={"tp": me - 1}, device_id_type=MESH,
        )

    @pl.when(me < n - 1)
    def _():
        rightward(me).start()

    @pl.when(me > 0)
    def _():
        leftward(me).start()

    def multiply(chunk, first):
        place = pl.ds(pl.multiple_of(chunk * length, length), length)

        def one(t, _):
            if first:
                pltpu.make_async_copy(
                    gate_w.at[:, pl.ds(0, TILE)], weights.at[t], weight_sem.at[t]
                ).wait()
            pre[t, place, :] = jnp.dot(
                rows[chunk], weights[t], preferred_element_type=jnp.float32
            ).astype(jnp.bfloat16)
            return 0

        lax.fori_loop(0, tiles, one, 0)
        step_raw[place, :] = jnp.dot(
            rows[chunk], step_buf[...], preferred_element_type=jnp.float32
        )

    step_copy.wait()
    multiply(me, True)
    for far in range(1, n):
        below, above = me - far, me + far

        @pl.when(below >= 0)
        def _():
            rightward(below).wait_recv()

            @pl.when(me < n - 1)
            def _():
                rightward(below).start()

        @pl.when(above < n)
        def _():
            leftward(above).wait_recv()

            @pl.when(me > 0)
            def _():
                leftward(above).start()

        @pl.when(below >= 0)
        def _():
            multiply(below, False)

        @pl.when(above < n)
        def _():
            multiply(above, False)

    for chunk in range(n):

        @pl.when(jnp.logical_and(chunk <= me, me < n - 1))
        def _():
            rightward(chunk).wait_send()

        @pl.when(jnp.logical_and(chunk >= me, me > 0))
        def _():
            leftward(chunk).wait_send()


def silu(v):
    return v / (1.0 + jnp.exp(-v))


def layer_kernel(
    n, slabs, value_tiles, key_tiles,
    pre, step_raw, value_conv, key_conv, query_conv, step_bias, decay_log, skip_gain, norm_gain, out_w,
    out,
    border, edge_buf, padded, keys, queries, scores, acts, cum_s, cum_t, step_t, tail_s, grow_s,
    grow_x, local0, slab, leaving, inflow, gated, squares, normed, weight, partial, from_left, from_right,
    edge_send, edge_recv, state_send, state_recv, weight_sem, part_send, left_recv, right_recv,
):
    me = lax.axis_index("tp")
    ctx = lax.axis_index("ctx")
    slab_rows, heads = step_raw.shape
    blocks = slab_rows // BLOCK
    length = slab_rows // n
    kernel_len = value_conv.shape[0]
    conv_tiles = value_tiles + 2 * key_tiles
    group_tiles = INNER // GROUPS // TILE
    width = TILE // (value_tiles * TILE // heads)
    last = slab_rows - 16
    pieces = partial.shape[1]
    piece = partial.shape[3]
    weight_copy = pltpu.make_async_copy(out_w, weight, weight_sem)
    weight_copy.start()
    for t in range(conv_tiles):
        edge_buf[t] = pre[value_tiles + t, pl.ds(last, 16), :]
    greet([
        ("tp", me - 1, me > 0), ("tp", me + 1, me < n - 1),
        ("ctx", ctx - 1, ctx > 0), ("ctx", ctx + 1, ctx < slabs - 1),
    ])
    edge = pltpu.make_async_remote_copy(
        src_ref=edge_buf, dst_ref=border, send_sem=edge_send, recv_sem=edge_recv,
        device_id={"ctx": ctx + 1}, device_id_type=MESH,
    )

    @pl.when(ctx < slabs - 1)
    def _():
        edge.start()

    @pl.when(ctx == 0)
    def _():
        border[...] = jnp.zeros_like(border)
        inflow[...] = jnp.zeros_like(inflow)

    row = lax.broadcasted_iota(jnp.int32, (BLOCK, BLOCK), 0)
    col = lax.broadcasted_iota(jnp.int32, (BLOCK, BLOCK), 1)
    causal = row >= col
    lower = jnp.where(causal, 1.0, 0.0)
    upper = jnp.where(row <= col, 1.0, 0.0)
    same = jnp.where(row == col, 1.0, 0.0)
    turned = (((0,), (0,)), ((), ()))
    raw = step_raw[...] + step_bias[...]
    step = jnp.maximum(raw, 0.0) + jnp.log1p(jnp.exp(-jnp.abs(raw)))
    rate = -jnp.exp(decay_log[...]) * step
    for b in range(blocks):
        lo = b * BLOCK
        rate_b, step_b = rate[lo:lo + BLOCK], step[lo:lo + BLOCK]
        cum = jnp.dot(lower, rate_b, precision=EXACT, preferred_element_type=jnp.float32)
        cum_s[pl.ds(lo, BLOCK), :] = cum
        cum_t[b] = lax.dot_general(rate_b, upper, turned, precision=EXACT, preferred_element_type=jnp.float32)
        step_t[b] = lax.dot_general(step_b, same, turned, precision=EXACT, preferred_element_type=jnp.float32)
        tail_s[pl.ds(lo, BLOCK), :] = jnp.exp(cum[BLOCK - 1:BLOCK] - cum) * step_b
        grow_s[pl.ds(lo, BLOCK), :] = jnp.exp(cum)

    def convolve(t, taps):
        padded[pl.ds(0, 16), :] = border[t].astype(jnp.float32)
        padded[pl.ds(16, slab_rows), :] = pre[value_tiles + t].astype(jnp.float32)
        total = padded[pl.ds(17 - kernel_len, slab_rows), :] * taps[0:1]
        for k in range(1, kernel_len):
            total = total + padded[pl.ds(17 - kernel_len + k, slab_rows), :] * taps[k:k + 1]
        return silu(total).astype(jnp.bfloat16)

    @pl.when(ctx > 0)
    def _():
        edge.wait_recv()

    per_tile = TILE // STATE
    for t in range(key_tiles):
        cols = slice(t * TILE, (t + 1) * TILE)
        key = convolve(value_tiles + t, key_conv[:, cols])
        query = convolve(value_tiles + key_tiles + t, query_conv[:, cols])
        for g in range(per_tile):
            keys[t * per_tile + g] = key[:, g * STATE:(g + 1) * STATE]
            queries[t * per_tile + g] = query[:, g * STATE:(g + 1) * STATE]
    for g in range(key_tiles * per_tile):
        for b in range(blocks):
            lo = b * BLOCK
            scores[g, b] = lax.dot_general(
                queries[g, pl.ds(lo, BLOCK), :], keys[g, pl.ds(lo, BLOCK), :],
                (((1,), (1,)), ((), ())), preferred_element_type=jnp.float32,
            )

    def spread(t, each, count):
        head = lax.broadcasted_iota(jnp.int32, (heads, each * count), 0)
        lane = lax.broadcasted_iota(jnp.int32, (heads, each * count), 1)
        return jnp.where(head == t * count + lane // each, 1.0, 0.0)

    def widen(array, matrix):
        return jnp.dot(array, matrix, precision=EXACT, preferred_element_type=jnp.float32)

    def state_copy(t):
        return pltpu.make_async_remote_copy(
            src_ref=leaving.at[t], dst_ref=inflow.at[t],
            send_sem=state_send.at[t], recv_sem=state_recv.at[t],
            device_id={"ctx": ctx + 1}, device_id_type=MESH,
        )

    def first_pass(t, _):
        place = pl.ds(pl.multiple_of(t * TILE, TILE), TILE)
        value = convolve(t, value_conv[:, place])
        acts[t] = value
        chooser = spread(t, TILE // width, width)
        tail = widen(tail_s[...], chooser)
        grow = widen(grow_s[...], chooser)
        grow_x[t] = grow
        weighted = (value.astype(jnp.float32) * tail).astype(jnp.bfloat16)
        g = t // group_tiles
        state = jnp.zeros((STATE, TILE), jnp.float32)
        for b in range(blocks):
            lo = b * BLOCK
            added = lax.dot_general(
                keys[g, pl.ds(lo, BLOCK), :], weighted[lo:lo + BLOCK], turned,
                preferred_element_type=jnp.float32,
            )
            state = grow[lo + BLOCK - 1:lo + BLOCK] * state + added
            if b < blocks - 1:
                local0[b, t] = state
        slab[t] = state

        @pl.when(ctx == 0)
        def _():
            leaving[t] = state.astype(jnp.bfloat16)
            if slabs > 1:
                state_copy(t).start()

        return 0

    lax.fori_loop(0, value_tiles, first_pass, 0)
    squares[...] = jnp.zeros_like(squares)
    left_half = lax.broadcasted_iota(jnp.int32, (BLOCK, BLOCK), 1) < TILE // width

    def second_pass(t, _):
        grow = grow_x[t]

        @pl.when(ctx > 0)
        def _():
            state_copy(t).wait_recv()

        start = inflow[t].astype(jnp.float32)
        fall = jnp.ones((1, TILE), jnp.float32)
        falls = []
        for b in range(blocks):
            falls.append(fall)
            fall = fall * grow[(b + 1) * BLOCK - 1:(b + 1) * BLOCK]

        @pl.when(jnp.logical_and(ctx > 0, ctx < slabs - 1))
        def _():
            leaving[t] = (fall * start + slab[t]).astype(jnp.bfloat16)
            state_copy(t).start()

        g = t // group_tiles
        columns = widen(cum_s[...], spread(t, BLOCK, width))
        place = pl.ds(pl.multiple_of(t * TILE, TILE), TILE)
        skip = widen(jnp.broadcast_to(skip_gain[...], (8, heads)), spread(t, TILE // width, width))[0:1]
        for b in range(blocks):
            lo = b * BLOCK
            value = acts[t, pl.ds(lo, BLOCK), :]
            parts = []
            for pair in range(width // 2):
                both = []
                for k in (2 * pair, 2 * pair + 1):
                    h = t * width + k
                    diff = columns[lo:lo + BLOCK, k * BLOCK:(k + 1) * BLOCK] - cum_t[b, pl.ds(h, 1), :]
                    factor = jnp.exp(jnp.where(causal, diff, -1e30))
                    mix = (scores[g, b] * factor * step_t[b, pl.ds(h, 1), :]).astype(jnp.bfloat16)
                    both.append(jnp.dot(
                        mix, value[:, pair * BLOCK:(pair + 1) * BLOCK], preferred_element_type=jnp.float32
                    ))
                parts.append(jnp.where(left_half, both[0], both[1]))
            inner = jnp.concatenate(parts, axis=1)
            enter = start if b == 0 else falls[b] * start + local0[b - 1, t]
            outer = jnp.dot(
                queries[g, pl.ds(lo, BLOCK), :], enter.astype(jnp.bfloat16), preferred_element_type=jnp.float32
            )
            ssm = inner + grow[lo:lo + BLOCK] * outer + skip * value.astype(jnp.float32)
            gate = pre[t, pl.ds(lo, BLOCK), :].astype(jnp.float32)
            result = ssm * silu(gate)
            gated[t, pl.ds(lo, BLOCK), :] = result
            squares[g, pl.ds(lo, BLOCK), :] += result * result
        return 0

    lax.fori_loop(0, value_tiles, second_pass, 0)
    groups_here = value_tiles // group_tiles
    for g in range(groups_here):
        scale = lax.rsqrt(jnp.sum(squares[g], axis=1, keepdims=True) / (INNER // GROUPS) + 1e-05)
        for t in range(g * group_tiles, (g + 1) * group_tiles):
            cols = slice(t * TILE, (t + 1) * TILE)
            normed[:, cols] = (gated[t] * scale * norm_gain[:, cols]).astype(jnp.bfloat16)

    weight_copy.wait()

    def product(b, p):
        rows = normed[pl.ds(pl.multiple_of(b * length, length), length), :]
        return jnp.dot(
            rows, weight[:, pl.ds(pl.multiple_of(p * piece, piece), piece)],
            preferred_element_type=jnp.float32,
        )

    def rightward(b, p):
        return pltpu.make_async_remote_copy(
            src_ref=partial.at[b, p], dst_ref=from_left.at[b, p],
            send_sem=part_send.at[b, p], recv_sem=left_recv.at[b, p],
            device_id={"tp": me + 1}, device_id_type=MESH,
        )

    def leftward(b, p):
        return pltpu.make_async_remote_copy(
            src_ref=partial.at[b, p], dst_ref=from_right.at[b, p],
            send_sem=part_send.at[b, p], recv_sem=right_recv.at[b, p],
            device_id={"tp": me - 1}, device_id_type=MESH,
        )

    for far in range(n - 1, 0, -1):
        above, below = me + far, me - far

        def forward(p, _):
            @pl.when(above < n)
            def _():
                mine = product(above, p)

                @pl.when(me == 0)
                def _():
                    partial[above, p] = mine.astype(jnp.bfloat16)

                @pl.when(me > 0)
                def _():
                    rightward(above, p).wait_recv()
                    partial[above, p] = (
                        mine + from_left[above, p].astype(jnp.float32)
                    ).astype(jnp.bfloat16)

                rightward(above, p).start()

            @pl.when(below >= 0)
            def _():
                mine = product(below, p)

                @pl.when(me == n - 1)
                def _():
                    partial[below, p] = mine.astype(jnp.bfloat16)

                @pl.when(me < n - 1)
                def _():
                    leftward(below, p).wait_recv()
                    partial[below, p] = (
                        mine + from_right[below, p].astype(jnp.float32)
                    ).astype(jnp.bfloat16)

                leftward(below, p).start()

            return 0

        lax.fori_loop(0, pieces, forward, 0)

    for p in range(pieces):
        cols = pl.ds(p * piece, piece)
        partial[me, p] = product(me, p).astype(jnp.bfloat16)

    @pl.when(me == 0)
    def _():
        from_left[me] = jnp.zeros(from_left.shape[1:], from_left.dtype)

    @pl.when(me == n - 1)
    def _():
        from_right[me] = jnp.zeros(from_right.shape[1:], from_right.dtype)

    for p in range(pieces):
        cols = pl.ds(p * piece, piece)

        @pl.when(me > 0)
        def _():
            rightward(me, p).wait_recv()

        @pl.when(me < n - 1)
        def _():
            leftward(me, p).wait_recv()

        out[:, cols] = (
            partial[me, p].astype(jnp.float32)
            + from_left[me, p].astype(jnp.float32)
            + from_right[me, p].astype(jnp.float32)
        ).astype(out.dtype)

    for b in range(n):

        @pl.when(b != me)
        def _():
            for p in range(pieces):
                rightward(b, p).wait_send()

    @pl.when(ctx < slabs - 1)
    def _():
        edge.wait_send()
        for t in range(value_tiles):
            state_copy(t).wait_send()


def fused(n, slabs, tokens, gate_weight, value_weight, key_weight, query_weight, step_weight,
          value_conv, key_conv, query_conv, step_bias, decay_log, skip_gain, norm_gain, out_weight):
    length, depth = tokens.shape
    columns = gate_weight.shape[1]
    key_cols = key_weight.shape[1]
    heads = step_weight.shape[1]
    slab_rows = length * n
    value_tiles, key_tiles = columns // TILE, key_cols // TILE
    tiles = 2 * value_tiles + 2 * key_tiles
    bf16, f32 = jnp.bfloat16, jnp.float32
    vmem, anywhere = pl.BlockSpec(memory_space=pltpu.VMEM), pl.BlockSpec(memory_space=pl.ANY)
    dma = pltpu.SemaphoreType.DMA
    pre, step_raw = pl.pallas_call(
        functools.partial(project_kernel, n, tiles),
        out_shape=(
            jax.ShapeDtypeStruct((tiles, slab_rows, TILE), bf16),
            jax.ShapeDtypeStruct((slab_rows, heads), f32),
        ),
        in_specs=[vmem] + [anywhere] * 5,
        out_specs=(vmem, vmem),
        scratch_shapes=[
            pltpu.VMEM((n, length, depth), bf16),
            pltpu.VMEM((tiles, depth, TILE), bf16),
            pltpu.VMEM((depth, heads), bf16),
            dma((tiles,)), dma, dma((n,)), dma((n,)), dma((n,)),
        ],
        compiler_params=pltpu.CompilerParams(
            collective_id=0, has_side_effects=True, vmem_limit_bytes=56 * 2**20
        ),
    )(tokens, gate_weight, value_weight, key_weight, query_weight, step_weight)
    blocks = slab_rows // BLOCK
    groups_here = key_cols // STATE
    out_cols = out_weight.shape[1]
    piece = 1024
    pieces = out_cols // piece
    wide = (value_tiles, slab_rows, TILE)
    conv_tiles = value_tiles + 2 * key_tiles
    return pl.pallas_call(
        functools.partial(layer_kernel, n, slabs, value_tiles, key_tiles),
        out_shape=jax.ShapeDtypeStruct((length, out_cols), bf16),
        in_specs=[vmem] * 9 + [anywhere],
        out_specs=vmem,
        scratch_shapes=[
            pltpu.VMEM((conv_tiles, 16, TILE), bf16),
            pltpu.VMEM((conv_tiles, 16, TILE), bf16),
            pltpu.VMEM((slab_rows + 16, TILE), f32),
            pltpu.VMEM((groups_here, slab_rows, STATE), bf16),
            pltpu.VMEM((groups_here, slab_rows, STATE), bf16),
            pltpu.VMEM((groups_here, blocks, BLOCK, BLOCK), f32),
            pltpu.VMEM(wide, bf16),
            pltpu.VMEM((slab_rows, heads), f32),
            pltpu.VMEM((blocks, heads, BLOCK), f32),
            pltpu.VMEM((blocks, heads, BLOCK), f32),
            pltpu.VMEM((slab_rows, heads), f32),
            pltpu.VMEM((slab_rows, heads), f32),
            pltpu.VMEM(wide, f32),
            pltpu.VMEM((max(blocks - 1, 1), value_tiles, STATE, TILE), f32),
            pltpu.VMEM((value_tiles, STATE, TILE), f32),
            pltpu.VMEM((value_tiles, STATE, TILE), bf16),
            pltpu.VMEM((value_tiles, STATE, TILE), bf16),
            pltpu.VMEM(wide, f32),
            pltpu.VMEM((groups_here, slab_rows, TILE), f32),
            pltpu.VMEM((slab_rows, columns), bf16),
            pltpu.VMEM(out_weight.shape, bf16),
            pltpu.VMEM((n, pieces, length, piece), bf16),
            pltpu.VMEM((n, pieces, length, piece), bf16),
            pltpu.VMEM((n, pieces, length, piece), bf16),
            dma, dma, dma((value_tiles,)), dma((value_tiles,)), dma,
            dma((n, pieces)), dma((n, pieces)), dma((n, pieces)),
        ],
        compiler_params=pltpu.CompilerParams(
            collective_id=1, has_side_effects=True, vmem_limit_bytes=56 * 2**20
        ),
    )(
        pre, step_raw, value_conv, key_conv, query_conv, step_bias[None], decay_log[None],
        skip_gain[None], norm_gain[None], out_weight,
    )


def solution(mesh):
    n, slabs = mesh.shape["tp"], mesh.shape["ctx"]
    whole_groups = INNER // n % (INNER // GROUPS) == 0 and GROUPS * STATE // n % TILE == 0
    body = functools.partial(fused, n, slabs) if whole_groups and n >= 4 else shards
    return jax.shard_map(
        body,
        mesh=mesh,
        in_specs=(
            P(("groups", "ctx", "tp"), None),
            P(None, "tp"),
            P(None, "tp"),
            P(None, "tp"),
            P(None, "tp"),
            P(None, "tp"),
            P(None, "tp"),
            P(None, "tp"),
            P(None, "tp"),
            P("tp"),
            P("tp"),
            P("tp"),
            P("tp"),
            P("tp", None),
        ),
        out_specs=P(("groups", "ctx", "tp"), None),
        check_vma=False,
    )
```

```python
import functools

import jax
import jax.numpy as jnp
from jax import lax
from jax.experimental import pallas as pl
from jax.experimental.pallas import tpu as pltpu
from jax.sharding import PartitionSpec as P

STATE = 128
GROUPS = 8
INNER = 8192


def passed_along(shard, axis, by):
    count = lax.axis_size(axis)
    pairs = [(i, i + by) for i in range(count) if 0 <= i + by < count]
    return lax.ppermute(shard, axis, pairs)


def from_partner(block, axis, distance):
    count = lax.axis_size(axis)
    route = []
    for low in range(count):
        high = low | 1 << distance
        if high != low and high < count:
            route += [(low, high), (high, low)]
    return lax.ppermute(block, axis, route)


def causal_mix(padded, kernel, length):
    total = padded[0:length] * kernel[0]
    for tap_index in range(1, kernel.shape[0]):
        total = total + padded[tap_index : tap_index + length] * kernel[tap_index]
    return total


def shards(
    tokens,
    gate_weight,
    value_weight,
    key_weight,
    query_weight,
    step_weight,
    value_conv,
    key_conv,
    query_conv,
    step_bias,
    decay_log,
    skip_gain,
    norm_gain,
    out_weight,
):
    tok_dev = tokens.shape[0]
    slab_rows = tok_dev * lax.axis_size("tp")
    columns = gate_weight.shape[1]
    key_cols = key_weight.shape[1]
    heads_here = step_weight.shape[1]
    head_width = columns // heads_here
    block_len = min(128, slab_rows)
    block_count = slab_rows // block_len
    kernel_len = value_conv.shape[0]
    joined = jnp.concatenate(
        [gate_weight, value_weight, key_weight, query_weight, step_weight], axis=1
    )
    projected = jnp.dot(
        lax.all_gather(tokens, "tp", axis=0, tiled=True), joined, preferred_element_type=jnp.float32
    )
    gate_in = projected[:, :columns].astype(jnp.bfloat16)
    mixed_pre = projected[:, columns : 2 * columns + 2 * key_cols].astype(jnp.bfloat16)
    step_raw = projected[:, 2 * columns + 2 * key_cols :]
    border = passed_along(mixed_pre[slab_rows - (kernel_len - 1) :], "ctx", 1)
    padded = jnp.concatenate([border, mixed_pre], axis=0).astype(jnp.float32)
    kernel = jnp.concatenate([value_conv, key_conv, query_conv], axis=1)
    activated = jax.nn.silu(causal_mix(padded, kernel, slab_rows)).astype(jnp.bfloat16)
    value_act = activated[:, :columns]
    key_act = activated[:, columns : columns + key_cols]
    query_act = activated[:, columns + key_cols :]
    group_cols = max(key_cols, STATE)
    reach = group_cols // key_cols
    key_group, query_group = (key_act, query_act)
    for bit_index in range(reach.bit_length() - 1):
        other_keys, other_queries = from_partner((key_group, query_group), "tp", bit_index)
        upper = lax.axis_index("tp") // (1 << bit_index) % 2 == 1
        key_group = jnp.where(
            upper,
            jnp.concatenate([other_keys, key_group], 1),
            jnp.concatenate([key_group, other_keys], 1),
        )
        query_group = jnp.where(
            upper,
            jnp.concatenate([other_queries, query_group], 1),
            jnp.concatenate([query_group, other_queries], 1),
        )
    local_groups = group_cols // STATE
    per_group = heads_here // local_groups
    step = jax.nn.softplus(step_raw + step_bias)
    rate = -jnp.exp(decay_log) * step
    cum = jnp.cumsum(rate.reshape(block_count, block_len, heads_here), axis=1)
    step_blk = step.reshape(block_count, block_len, heads_here)
    values = value_act.reshape(block_count, block_len, heads_here, head_width)
    keys = key_group.reshape(block_count, block_len, local_groups, STATE)
    queries = query_group.reshape(block_count, block_len, local_groups, STATE)
    scores = jnp.einsum("btgn,bugn->gbtu", queries, keys, preferred_element_type=jnp.float32)
    scores = jnp.repeat(scores, per_group, axis=0)
    cum_t = jnp.transpose(cum, (2, 0, 1))
    step_t = jnp.transpose(step_blk, (2, 0, 1))
    causal = jnp.tril(jnp.ones((block_len, block_len), jnp.bool_))
    diff = cum_t[:, :, :, None] - cum_t[:, :, None, :]
    factor = jnp.where(causal, jnp.exp(jnp.where(causal, diff, 0.0)), 0.0)
    weights = (scores * factor * step_t[:, :, None, :]).astype(jnp.bfloat16)
    inner = jnp.einsum("hbtu,buhp->bthp", weights, values, preferred_element_type=jnp.float32)
    tail = jnp.exp(cum[:, -1:, :] - cum) * step_blk
    weighted = (values * tail[:, :, :, None]).astype(jnp.bfloat16)
    key_heads = jnp.repeat(keys, per_group, axis=2)
    query_heads = jnp.repeat(queries, per_group, axis=2)
    local = jnp.einsum("buhn,buhp->bhnp", key_heads, weighted, preferred_element_type=jnp.float32)
    falloff = jnp.exp(cum[:, -1, :])

    def advance(carry, item):
        fade, added = item
        return (fade[:, None, None] * carry + added, carry)

    zero_state = jnp.zeros((heads_here, STATE, head_width), jnp.float32)
    slab_state, _ = lax.scan(advance, zero_state, (falloff, local))
    slab_fall = jnp.exp(jnp.sum(cum[:, -1, :], axis=0))
    inflow = zero_state
    for turn in range(lax.axis_size("ctx") - 1):
        inflow = passed_along(
            (slab_fall[:, None, None] * inflow + slab_state).astype(jnp.bfloat16), "ctx", 1
        ).astype(jnp.float32)
    _, starts = lax.scan(advance, inflow, (falloff, local))
    outer = jnp.einsum(
        "bthn,bhnp->bthp", query_heads.astype(jnp.float32), starts, precision=lax.Precision.HIGHEST
    )
    ssm_out = (
        inner
        + jnp.exp(cum)[:, :, :, None] * outer
        + skip_gain[:, None] * values.astype(jnp.float32)
    )
    ssm_out = ssm_out.reshape(slab_rows, columns)
    gated = ssm_out * jax.nn.silu(gate_in.astype(jnp.float32))
    span = INNER // GROUPS
    piece_len = min(columns, span)
    norm_here = columns // piece_len
    squares = jnp.sum((gated * gated).reshape(slab_rows, norm_here, piece_len), axis=2)
    norm_reach = span // piece_len
    for bit_index in range(norm_reach.bit_length() - 1):
        squares = squares + from_partner(squares, "tp", bit_index)
    scale = lax.rsqrt(squares / span + 1e-05)
    normed = (gated.reshape(slab_rows, norm_here, piece_len) * scale[:, :, None]).reshape(
        slab_rows, columns
    ) * norm_gain
    normed = normed.astype(jnp.bfloat16)
    return lax.psum_scatter(
        jnp.dot(normed, out_weight, preferred_element_type=jnp.float32).astype(jnp.bfloat16),
        "tp",
        scatter_dimension=0,
        tiled=True,
    )


TILE = 256
BLOCK = 128
MESH = pl.DeviceIdType.MESH
EXACT = lax.Precision.HIGHEST


def greet(neighbours):
    barrier = pltpu.get_barrier_semaphore()
    count = 0
    for axis, index, exists in neighbours:

        @pl.when(exists)
        def _():
            pl.semaphore_signal(barrier, inc=1, device_id={axis: index}, device_id_type=MESH)

        count = count + exists.astype(jnp.int32)
    pl.semaphore_wait(barrier, count)


def project_kernel(
    n, tiles, quarters, tokens, gate_w, value_w, key_w, query_w, step_w, pre, step_raw,
    rows, weights, step_buf, total, step_total,
    weight_sem, step_sem, send_left, send_right, recv_sem,
):
    me = lax.axis_index("tp")
    length, depth = tokens.shape
    deep = depth // quarters
    step_copy = pltpu.make_async_copy(step_w, step_buf, step_sem)
    step_copy.start()
    for q in range(quarters):
        tile = 0
        for source in (gate_w, value_w, key_w, query_w):
            for part in range(source.shape[1] // TILE):
                pltpu.make_async_copy(
                    source.at[pl.ds(q * deep, deep), pl.ds(part * TILE, TILE)],
                    weights.at[q, tile], weight_sem.at[q, tile],
                ).start()
                tile += 1

    def place(chunk):
        return pl.ds(pl.multiple_of(chunk * length, length), length)

    for q in range(quarters):
        rows[q, place(me), :] = tokens[:, q * deep:(q + 1) * deep]
    greet([("tp", me - 1, me > 0), ("tp", me + 1, me < n - 1)])

    def rightward(q, chunk):
        spot = rows.at[q, place(chunk)]
        return pltpu.make_async_remote_copy(
            src_ref=spot, dst_ref=spot,
            send_sem=send_right.at[q, chunk], recv_sem=recv_sem.at[q, chunk],
            device_id={"tp": me + 1}, device_id_type=MESH,
        )

    def leftward(q, chunk):
        spot = rows.at[q, place(chunk)]
        return pltpu.make_async_remote_copy(
            src_ref=spot, dst_ref=spot,
            send_sem=send_left.at[q, chunk], recv_sem=recv_sem.at[q, chunk],
            device_id={"tp": me - 1}, device_id_type=MESH,
        )

    for q in range(quarters):

        @pl.when(me < n - 1)
        def _():
            rightward(q, me).start()

        @pl.when(me > 0)
        def _():
            leftward(q, me).start()

    def receive(q, far):
        below, above = me - far, me + far

        @pl.when(below >= 0)
        def _():
            rightward(q, below).wait_recv()

            @pl.when(me < n - 1)
            def _():
                rightward(q, below).start()

        @pl.when(above < n)
        def _():
            leftward(q, above).wait_recv()

            @pl.when(me > 0)
            def _():
                leftward(q, above).start()

    for far in range(1, n - 1):
        for q in range(quarters):
            receive(q, far)
    step_copy.wait()
    for q in range(quarters):
        receive(q, n - 1)

        def one(t, _):
            pltpu.make_async_copy(
                gate_w.at[pl.ds(0, deep), pl.ds(0, TILE)], weights.at[q, t], weight_sem.at[q, t]
            ).wait()
            added = jnp.dot(rows[q], weights[q, t], preferred_element_type=jnp.float32)
            if q > 0:
                added = total[t] + added
            if q < quarters - 1:
                total[t] = added
            else:
                pre[t] = added.astype(jnp.bfloat16)
            return 0

        lax.fori_loop(0, tiles, one, 0)
        added = lax.dot_general(
            rows[q], step_buf[:, q * deep:(q + 1) * deep], (((1,), (1,)), ((), ())),
            preferred_element_type=jnp.float32,
        )
        if q > 0:
            added = step_total[...] + added
        if q < quarters - 1:
            step_total[...] = added
        else:
            step_raw[...] = added

    for q in range(quarters):
        for chunk in range(n):

            @pl.when(jnp.logical_and(chunk <= me, me < n - 1))
            def _():
                rightward(q, chunk).wait_send()

            @pl.when(jnp.logical_and(chunk >= me, me > 0))
            def _():
                leftward(q, chunk).wait_send()


def silu(v):
    return v / (1.0 + jnp.exp(-v))


def three_parts(array):
    high = array.astype(jnp.bfloat16)
    rest = array - high.astype(jnp.float32)
    middle = rest.astype(jnp.bfloat16)
    low = (rest - middle.astype(jnp.float32)).astype(jnp.bfloat16)
    return jnp.concatenate([high, middle, low], axis=1)


def layer_kernel(
    n, slabs, value_tiles, key_tiles,
    pre, step_raw, value_conv, key_conv, query_conv, step_bias, decay_log, skip_gain, norm_gain, out_w,
    out,
    border, edge_buf, padded, keys, queries, scores, acts, cum_s, cum_t, step_t, tail_s, grow_s,
    grow_x, local0, slab, leaving, inflow, gated, squares, normed, weight, partial, from_left, from_right,
    edge_send, edge_recv, state_send, state_recv, weight_sem, part_send, left_recv, right_recv,
):
    me = lax.axis_index("tp")
    ctx = lax.axis_index("ctx")
    slab_rows, heads = step_raw.shape
    blocks = slab_rows // BLOCK
    length = slab_rows // n
    kernel_len = value_conv.shape[0]
    conv_tiles = value_tiles + 2 * key_tiles
    group_tiles = INNER // GROUPS // TILE
    width = TILE // (value_tiles * TILE // heads)
    last = slab_rows - 16
    pieces = partial.shape[1]
    piece = partial.shape[3]
    weight_copy = pltpu.make_async_copy(out_w, weight, weight_sem)
    weight_copy.start()
    for t in range(conv_tiles):
        edge_buf[t] = pre[value_tiles + t, pl.ds(last, 16), :]
    greet([
        ("tp", me - 1, me > 0), ("tp", me + 1, me < n - 1),
        ("ctx", ctx - 1, ctx > 0), ("ctx", ctx + 1, ctx < slabs - 1),
    ])
    edge = pltpu.make_async_remote_copy(
        src_ref=edge_buf, dst_ref=border, send_sem=edge_send, recv_sem=edge_recv,
        device_id={"ctx": ctx + 1}, device_id_type=MESH,
    )

    @pl.when(ctx < slabs - 1)
    def _():
        edge.start()

    @pl.when(ctx == 0)
    def _():
        border[...] = jnp.zeros_like(border)
        inflow[...] = jnp.zeros_like(inflow)

    row = lax.broadcasted_iota(jnp.int32, (BLOCK, BLOCK), 0)
    col = lax.broadcasted_iota(jnp.int32, (BLOCK, BLOCK), 1)
    causal = row >= col
    lower = jnp.where(causal, 1.0, 0.0)
    upper = jnp.where(row <= col, 1.0, 0.0)
    same = jnp.where(row == col, 1.0, 0.0)
    turned = (((0,), (0,)), ((), ()))
    raw = step_raw[...] + step_bias[...]
    step = jnp.maximum(raw, 0.0) + jnp.log1p(jnp.exp(-jnp.abs(raw)))
    rate = -jnp.exp(decay_log[...]) * step
    for b in range(blocks):
        lo = b * BLOCK
        rate_b, step_b = rate[lo:lo + BLOCK], step[lo:lo + BLOCK]
        cum = jnp.dot(lower, rate_b, precision=EXACT, preferred_element_type=jnp.float32)
        cum_s[pl.ds(lo, BLOCK), :] = three_parts(cum)
        cum_t[b] = lax.dot_general(rate_b, upper, turned, precision=EXACT, preferred_element_type=jnp.float32)
        step_t[b] = lax.dot_general(step_b, same, turned, precision=EXACT, preferred_element_type=jnp.float32)
        tail_s[pl.ds(lo, BLOCK), :] = three_parts(jnp.exp(cum[BLOCK - 1:BLOCK] - cum) * step_b)
        grow_s[pl.ds(lo, BLOCK), :] = three_parts(jnp.exp(cum))

    def convolve(t, taps):
        padded[pl.ds(0, 16), :] = border[t].astype(jnp.float32)
        padded[pl.ds(16, slab_rows), :] = pre[value_tiles + t].astype(jnp.float32)
        total = padded[pl.ds(17 - kernel_len, slab_rows), :] * taps[0:1]
        for k in range(1, kernel_len):
            total = total + padded[pl.ds(17 - kernel_len + k, slab_rows), :] * taps[k:k + 1]
        return silu(total).astype(jnp.bfloat16)

    @pl.when(ctx > 0)
    def _():
        edge.wait_recv()

    per_tile = TILE // STATE
    for t in range(key_tiles):
        cols = slice(t * TILE, (t + 1) * TILE)
        key = convolve(value_tiles + t, key_conv[:, cols])
        query = convolve(value_tiles + key_tiles + t, query_conv[:, cols])
        for g in range(per_tile):
            keys[t * per_tile + g] = key[:, g * STATE:(g + 1) * STATE]
            queries[t * per_tile + g] = query[:, g * STATE:(g + 1) * STATE]
    for g in range(key_tiles * per_tile):
        for b in range(blocks):
            lo = b * BLOCK
            scores[g, b] = lax.dot_general(
                queries[g, pl.ds(lo, BLOCK), :], keys[g, pl.ds(lo, BLOCK), :],
                (((1,), (1,)), ((), ())), preferred_element_type=jnp.float32,
            )

    def spread(t, each, count):
        head = lax.broadcasted_iota(jnp.int32, (3 * heads, each * count), 0) % heads
        lane = lax.broadcasted_iota(jnp.int32, (3 * heads, each * count), 1)
        return jnp.where(head == t * count + lane // each, 1.0, 0.0).astype(jnp.bfloat16)

    def widen(array, matrix):
        return jnp.dot(array, matrix, preferred_element_type=jnp.float32)

    def state_copy(t):
        return pltpu.make_async_remote_copy(
            src_ref=leaving.at[t], dst_ref=inflow.at[t],
            send_sem=state_send.at[t], recv_sem=state_recv.at[t],
            device_id={"ctx": ctx + 1}, device_id_type=MESH,
        )

    def first_pass(t, _):
        place = pl.ds(pl.multiple_of(t * TILE, TILE), TILE)
        value = convolve(t, value_conv[:, place])
        acts[t] = value
        chooser = spread(t, TILE // width, width)
        tail = widen(tail_s[...], chooser)
        grow = widen(grow_s[...], chooser)
        grow_x[t] = grow
        weighted = (value.astype(jnp.float32) * tail).astype(jnp.bfloat16)
        g = t // group_tiles
        state = jnp.zeros((STATE, TILE), jnp.float32)
        for b in range(blocks):
            lo = b * BLOCK
            added = lax.dot_general(
                keys[g, pl.ds(lo, BLOCK), :], weighted[lo:lo + BLOCK], turned,
                preferred_element_type=jnp.float32,
            )
            state = grow[lo + BLOCK - 1:lo + BLOCK] * state + added
            if b < blocks - 1:
                local0[b, t] = state
        slab[t] = state

        @pl.when(ctx == 0)
        def _():
            leaving[t] = state.astype(jnp.bfloat16)
            if slabs > 1:
                state_copy(t).start()

        return 0

    lax.fori_loop(0, value_tiles, first_pass, 0)
    squares[...] = jnp.zeros_like(squares)
    skip_parts = three_parts(jnp.broadcast_to(skip_gain[...], (16, heads)))
    left_half = lax.broadcasted_iota(jnp.int32, (BLOCK, BLOCK), 1) < TILE // width

    def second_pass(t, _):
        grow = grow_x[t]

        @pl.when(ctx > 0)
        def _():
            state_copy(t).wait_recv()

        start = inflow[t].astype(jnp.float32)
        fall = jnp.ones((1, TILE), jnp.float32)
        falls = []
        for b in range(blocks):
            falls.append(fall)
            fall = fall * grow[(b + 1) * BLOCK - 1:(b + 1) * BLOCK]

        @pl.when(jnp.logical_and(ctx > 0, ctx < slabs - 1))
        def _():
            leaving[t] = (fall * start + slab[t]).astype(jnp.bfloat16)
            state_copy(t).start()

        g = t // group_tiles
        columns = widen(cum_s[...], spread(t, BLOCK, width))
        place = pl.ds(pl.multiple_of(t * TILE, TILE), TILE)
        skip = widen(skip_parts, spread(t, TILE // width, width))[0:1]
        for b in range(blocks):
            lo = b * BLOCK
            value = acts[t, pl.ds(lo, BLOCK), :]
            parts = []
            for pair in range(width // 2):
                both = []
                for k in (2 * pair, 2 * pair + 1):
                    h = t * width + k
                    diff = columns[lo:lo + BLOCK, k * BLOCK:(k + 1) * BLOCK] - cum_t[b, pl.ds(h, 1), :]
                    factor = jnp.exp(jnp.where(causal, diff, -1e30))
                    mix = (scores[g, b] * factor * step_t[b, pl.ds(h, 1), :]).astype(jnp.bfloat16)
                    both.append(jnp.dot(
                        mix, value[:, pair * BLOCK:(pair + 1) * BLOCK], preferred_element_type=jnp.float32
                    ))
                parts.append(jnp.where(left_half, both[0], both[1]))
            inner = jnp.concatenate(parts, axis=1)
            enter = start if b == 0 else falls[b] * start + local0[b - 1, t]
            outer = jnp.dot(
                queries[g, pl.ds(lo, BLOCK), :], enter.astype(jnp.bfloat16), preferred_element_type=jnp.float32
            )
            ssm = inner + grow[lo:lo + BLOCK] * outer + skip * value.astype(jnp.float32)
            gate = pre[t, pl.ds(lo, BLOCK), :].astype(jnp.float32)
            result = ssm * silu(gate)
            gated[t, pl.ds(lo, BLOCK), :] = result
            squares[g, pl.ds(lo, BLOCK), :] += result * result
        return 0

    lax.fori_loop(0, value_tiles, second_pass, 0)
    groups_here = value_tiles // group_tiles
    for g in range(groups_here):
        scale = lax.rsqrt(jnp.sum(squares[g], axis=1, keepdims=True) / (INNER // GROUPS) + 1e-05)
        for t in range(g * group_tiles, (g + 1) * group_tiles):
            cols = slice(t * TILE, (t + 1) * TILE)
            normed[:, cols] = (gated[t] * scale * norm_gain[:, cols]).astype(jnp.bfloat16)

    weight_copy.wait()

    def product(b, p):
        rows = normed[pl.ds(pl.multiple_of(b * length, length), length), :]
        return jnp.dot(
            rows, weight[:, pl.ds(pl.multiple_of(p * piece, piece), piece)],
            preferred_element_type=jnp.float32,
        )

    def rightward(b, p):
        return pltpu.make_async_remote_copy(
            src_ref=partial.at[b, p], dst_ref=from_left.at[b, p],
            send_sem=part_send.at[b, p], recv_sem=left_recv.at[b, p],
            device_id={"tp": me + 1}, device_id_type=MESH,
        )

    def leftward(b, p):
        return pltpu.make_async_remote_copy(
            src_ref=partial.at[b, p], dst_ref=from_right.at[b, p],
            send_sem=part_send.at[b, p], recv_sem=right_recv.at[b, p],
            device_id={"tp": me - 1}, device_id_type=MESH,
        )

    for far in range(n - 1, 0, -1):
        above, below = me + far, me - far

        def forward(p, _):
            @pl.when(above < n)
            def _():
                mine = product(above, p)

                @pl.when(me == 0)
                def _():
                    partial[above, p] = mine.astype(jnp.bfloat16)

                @pl.when(me > 0)
                def _():
                    rightward(above, p).wait_recv()
                    partial[above, p] = (
                        mine + from_left[above, p].astype(jnp.float32)
                    ).astype(jnp.bfloat16)

                rightward(above, p).start()

            @pl.when(below >= 0)
            def _():
                mine = product(below, p)

                @pl.when(me == n - 1)
                def _():
                    partial[below, p] = mine.astype(jnp.bfloat16)

                @pl.when(me < n - 1)
                def _():
                    leftward(below, p).wait_recv()
                    partial[below, p] = (
                        mine + from_right[below, p].astype(jnp.float32)
                    ).astype(jnp.bfloat16)

                leftward(below, p).start()

            return 0

        lax.fori_loop(0, pieces, forward, 0)

    for p in range(pieces):
        cols = pl.ds(p * piece, piece)
        partial[me, p] = product(me, p).astype(jnp.bfloat16)

    @pl.when(me == 0)
    def _():
        from_left[me] = jnp.zeros(from_left.shape[1:], from_left.dtype)

    @pl.when(me == n - 1)
    def _():
        from_right[me] = jnp.zeros(from_right.shape[1:], from_right.dtype)

    for p in range(pieces):
        cols = pl.ds(p * piece, piece)

        @pl.when(me > 0)
        def _():
            rightward(me, p).wait_recv()

        @pl.when(me < n - 1)
        def _():
            leftward(me, p).wait_recv()

        out[:, cols] = (
            partial[me, p].astype(jnp.float32)
            + from_left[me, p].astype(jnp.float32)
            + from_right[me, p].astype(jnp.float32)
        ).astype(out.dtype)

    for b in range(n):

        @pl.when(b != me)
        def _():
            for p in range(pieces):
                rightward(b, p).wait_send()

    @pl.when(ctx < slabs - 1)
    def _():
        edge.wait_send()
        for t in range(value_tiles):
            state_copy(t).wait_send()


def fused(n, slabs, tokens, gate_weight, value_weight, key_weight, query_weight, step_weight,
          value_conv, key_conv, query_conv, step_bias, decay_log, skip_gain, norm_gain, out_weight):
    length, depth = tokens.shape
    columns = gate_weight.shape[1]
    key_cols = key_weight.shape[1]
    heads = step_weight.shape[1]
    slab_rows = length * n
    value_tiles, key_tiles = columns // TILE, key_cols // TILE
    tiles = 2 * value_tiles + 2 * key_tiles
    quarters = 4
    deep = depth // quarters
    bf16, f32 = jnp.bfloat16, jnp.float32
    vmem, anywhere = pl.BlockSpec(memory_space=pltpu.VMEM), pl.BlockSpec(memory_space=pl.ANY)
    dma = pltpu.SemaphoreType.DMA
    pre, step_raw = pl.pallas_call(
        functools.partial(project_kernel, n, tiles, quarters),
        out_shape=(
            jax.ShapeDtypeStruct((tiles, slab_rows, TILE), bf16),
            jax.ShapeDtypeStruct((slab_rows, heads), f32),
        ),
        in_specs=[vmem] + [anywhere] * 5,
        out_specs=(vmem, vmem),
        scratch_shapes=[
            pltpu.VMEM((quarters, slab_rows, deep), bf16),
            pltpu.VMEM((quarters, tiles, deep, TILE), bf16),
            pltpu.VMEM((heads, depth), bf16),
            pltpu.VMEM((tiles, slab_rows, TILE), f32),
            pltpu.VMEM((slab_rows, heads), f32),
            dma((quarters, tiles)), dma, dma((quarters, n)), dma((quarters, n)), dma((quarters, n)),
        ],
        compiler_params=pltpu.CompilerParams(
            collective_id=0, has_side_effects=True, vmem_limit_bytes=56 * 2**20
        ),
    )(tokens, gate_weight, value_weight, key_weight, query_weight, step_weight.T)
    blocks = slab_rows // BLOCK
    groups_here = key_cols // STATE
    out_cols = out_weight.shape[1]
    piece = 1024
    pieces = out_cols // piece
    wide = (value_tiles, slab_rows, TILE)
    conv_tiles = value_tiles + 2 * key_tiles
    return pl.pallas_call(
        functools.partial(layer_kernel, n, slabs, value_tiles, key_tiles),
        out_shape=jax.ShapeDtypeStruct((length, out_cols), f32),
        in_specs=[vmem] * 9 + [anywhere],
        out_specs=vmem,
        scratch_shapes=[
            pltpu.VMEM((conv_tiles, 16, TILE), bf16),
            pltpu.VMEM((conv_tiles, 16, TILE), bf16),
            pltpu.VMEM((slab_rows + 16, TILE), f32),
            pltpu.VMEM((groups_here, slab_rows, STATE), bf16),
            pltpu.VMEM((groups_here, slab_rows, STATE), bf16),
            pltpu.VMEM((groups_here, blocks, BLOCK, BLOCK), f32),
            pltpu.VMEM(wide, bf16),
            pltpu.VMEM((slab_rows, 3 * heads), bf16),
            pltpu.VMEM((blocks, heads, BLOCK), f32),
            pltpu.VMEM((blocks, heads, BLOCK), f32),
            pltpu.VMEM((slab_rows, 3 * heads), bf16),
            pltpu.VMEM((slab_rows, 3 * heads), bf16),
            pltpu.VMEM(wide, f32),
            pltpu.VMEM((max(blocks - 1, 1), value_tiles, STATE, TILE), f32),
            pltpu.VMEM((value_tiles, STATE, TILE), f32),
            pltpu.VMEM((value_tiles, STATE, TILE), bf16),
            pltpu.VMEM((value_tiles, STATE, TILE), bf16),
            pltpu.VMEM(wide, f32),
            pltpu.VMEM((groups_here, slab_rows, TILE), f32),
            pltpu.VMEM((slab_rows, columns), bf16),
            pltpu.VMEM(out_weight.shape, bf16),
            pltpu.VMEM((n, pieces, length, piece), bf16),
            pltpu.VMEM((n, pieces, length, piece), bf16),
            pltpu.VMEM((n, pieces, length, piece), bf16),
            dma, dma, dma((value_tiles,)), dma((value_tiles,)), dma,
            dma((n, pieces)), dma((n, pieces)), dma((n, pieces)),
        ],
        compiler_params=pltpu.CompilerParams(
            collective_id=1, has_side_effects=True, vmem_limit_bytes=56 * 2**20
        ),
    )(
        pre, step_raw, value_conv, key_conv, query_conv, step_bias[None], decay_log[None],
        skip_gain[None], norm_gain[None], out_weight,
    ).astype(bf16)


def solution(mesh):
    n, slabs = mesh.shape["tp"], mesh.shape["ctx"]
    whole_groups = INNER // n % (INNER // GROUPS) == 0 and GROUPS * STATE // n % TILE == 0
    body = functools.partial(fused, n, slabs) if whole_groups and n >= 4 else shards
    return jax.shard_map(
        body,
        mesh=mesh,
        in_specs=(
            P(("groups", "ctx", "tp"), None),
            P(None, "tp"),
            P(None, "tp"),
            P(None, "tp"),
            P(None, "tp"),
            P(None, "tp"),
            P(None, "tp"),
            P(None, "tp"),
            P(None, "tp"),
            P("tp"),
            P("tp"),
            P("tp"),
            P("tp"),
            P("tp", None),
        ),
        out_specs=P(("groups", "ctx", "tp"), None),
        check_vma=False,
    )
```

```python
import functools

import jax
import jax.numpy as jnp
from jax import lax
from jax.experimental import pallas as pl
from jax.experimental.pallas import tpu as pltpu
from jax.sharding import PartitionSpec as P

STATE = 128
GROUPS = 8
INNER = 8192


def passed_along(shard, axis, by):
    count = lax.axis_size(axis)
    pairs = [(i, i + by) for i in range(count) if 0 <= i + by < count]
    return lax.ppermute(shard, axis, pairs)


def from_partner(block, axis, distance):
    count = lax.axis_size(axis)
    route = []
    for low in range(count):
        high = low | 1 << distance
        if high != low and high < count:
            route += [(low, high), (high, low)]
    return lax.ppermute(block, axis, route)


def causal_mix(padded, kernel, length):
    total = padded[0:length] * kernel[0]
    for tap_index in range(1, kernel.shape[0]):
        total = total + padded[tap_index : tap_index + length] * kernel[tap_index]
    return total


def shards(
    tokens,
    gate_weight,
    value_weight,
    key_weight,
    query_weight,
    step_weight,
    value_conv,
    key_conv,
    query_conv,
    step_bias,
    decay_log,
    skip_gain,
    norm_gain,
    out_weight,
):
    tok_dev = tokens.shape[0]
    slab_rows = tok_dev * lax.axis_size("tp")
    columns = gate_weight.shape[1]
    key_cols = key_weight.shape[1]
    heads_here = step_weight.shape[1]
    head_width = columns // heads_here
    block_len = min(128, slab_rows)
    block_count = slab_rows // block_len
    kernel_len = value_conv.shape[0]
    joined = jnp.concatenate(
        [gate_weight, value_weight, key_weight, query_weight, step_weight], axis=1
    )
    projected = jnp.dot(
        lax.all_gather(tokens, "tp", axis=0, tiled=True), joined, preferred_element_type=jnp.float32
    )
    gate_in = projected[:, :columns].astype(jnp.bfloat16)
    mixed_pre = projected[:, columns : 2 * columns + 2 * key_cols].astype(jnp.bfloat16)
    step_raw = projected[:, 2 * columns + 2 * key_cols :]
    border = passed_along(mixed_pre[slab_rows - (kernel_len - 1) :], "ctx", 1)
    padded = jnp.concatenate([border, mixed_pre], axis=0).astype(jnp.float32)
    kernel = jnp.concatenate([value_conv, key_conv, query_conv], axis=1)
    activated = jax.nn.silu(causal_mix(padded, kernel, slab_rows)).astype(jnp.bfloat16)
    value_act = activated[:, :columns]
    key_act = activated[:, columns : columns + key_cols]
    query_act = activated[:, columns + key_cols :]
    group_cols = max(key_cols, STATE)
    reach = group_cols // key_cols
    key_group, query_group = (key_act, query_act)
    for bit_index in range(reach.bit_length() - 1):
        other_keys, other_queries = from_partner((key_group, query_group), "tp", bit_index)
        upper = lax.axis_index("tp") // (1 << bit_index) % 2 == 1
        key_group = jnp.where(
            upper,
            jnp.concatenate([other_keys, key_group], 1),
            jnp.concatenate([key_group, other_keys], 1),
        )
        query_group = jnp.where(
            upper,
            jnp.concatenate([other_queries, query_group], 1),
            jnp.concatenate([query_group, other_queries], 1),
        )
    local_groups = group_cols // STATE
    per_group = heads_here // local_groups
    step = jax.nn.softplus(step_raw + step_bias)
    rate = -jnp.exp(decay_log) * step
    cum = jnp.cumsum(rate.reshape(block_count, block_len, heads_here), axis=1)
    step_blk = step.reshape(block_count, block_len, heads_here)
    values = value_act.reshape(block_count, block_len, heads_here, head_width)
    keys = key_group.reshape(block_count, block_len, local_groups, STATE)
    queries = query_group.reshape(block_count, block_len, local_groups, STATE)
    scores = jnp.einsum("btgn,bugn->gbtu", queries, keys, preferred_element_type=jnp.float32)
    scores = jnp.repeat(scores, per_group, axis=0)
    cum_t = jnp.transpose(cum, (2, 0, 1))
    step_t = jnp.transpose(step_blk, (2, 0, 1))
    causal = jnp.tril(jnp.ones((block_len, block_len), jnp.bool_))
    diff = cum_t[:, :, :, None] - cum_t[:, :, None, :]
    factor = jnp.where(causal, jnp.exp(jnp.where(causal, diff, 0.0)), 0.0)
    weights = (scores * factor * step_t[:, :, None, :]).astype(jnp.bfloat16)
    inner = jnp.einsum("hbtu,buhp->bthp", weights, values, preferred_element_type=jnp.float32)
    tail = jnp.exp(cum[:, -1:, :] - cum) * step_blk
    weighted = (values * tail[:, :, :, None]).astype(jnp.bfloat16)
    key_heads = jnp.repeat(keys, per_group, axis=2)
    query_heads = jnp.repeat(queries, per_group, axis=2)
    local = jnp.einsum("buhn,buhp->bhnp", key_heads, weighted, preferred_element_type=jnp.float32)
    falloff = jnp.exp(cum[:, -1, :])

    def advance(carry, item):
        fade, added = item
        return (fade[:, None, None] * carry + added, carry)

    zero_state = jnp.zeros((heads_here, STATE, head_width), jnp.float32)
    slab_state, _ = lax.scan(advance, zero_state, (falloff, local))
    slab_fall = jnp.exp(jnp.sum(cum[:, -1, :], axis=0))
    inflow = zero_state
    for turn in range(lax.axis_size("ctx") - 1):
        inflow = passed_along(
            (slab_fall[:, None, None] * inflow + slab_state).astype(jnp.bfloat16), "ctx", 1
        ).astype(jnp.float32)
    _, starts = lax.scan(advance, inflow, (falloff, local))
    outer = jnp.einsum(
        "bthn,bhnp->bthp", query_heads.astype(jnp.float32), starts, precision=lax.Precision.HIGHEST
    )
    ssm_out = (
        inner
        + jnp.exp(cum)[:, :, :, None] * outer
        + skip_gain[:, None] * values.astype(jnp.float32)
    )
    ssm_out = ssm_out.reshape(slab_rows, columns)
    gated = ssm_out * jax.nn.silu(gate_in.astype(jnp.float32))
    span = INNER // GROUPS
    piece_len = min(columns, span)
    norm_here = columns // piece_len
    squares = jnp.sum((gated * gated).reshape(slab_rows, norm_here, piece_len), axis=2)
    norm_reach = span // piece_len
    for bit_index in range(norm_reach.bit_length() - 1):
        squares = squares + from_partner(squares, "tp", bit_index)
    scale = lax.rsqrt(squares / span + 1e-05)
    normed = (gated.reshape(slab_rows, norm_here, piece_len) * scale[:, :, None]).reshape(
        slab_rows, columns
    ) * norm_gain
    normed = normed.astype(jnp.bfloat16)
    return lax.psum_scatter(
        jnp.dot(normed, out_weight, preferred_element_type=jnp.float32).astype(jnp.bfloat16),
        "tp",
        scatter_dimension=0,
        tiled=True,
    )


TILE = 256
BLOCK = 128
MESH = pl.DeviceIdType.MESH
EXACT = lax.Precision.HIGHEST


def greet(neighbours):
    barrier = pltpu.get_barrier_semaphore()
    count = 0
    for axis, index, exists in neighbours:

        @pl.when(exists)
        def _():
            pl.semaphore_signal(barrier, inc=1, device_id={axis: index}, device_id_type=MESH)

        count = count + exists.astype(jnp.int32)
    pl.semaphore_wait(barrier, count)


def project_kernel(
    n, tiles, quarters, tokens, gate_w, value_w, key_w, query_w, step_w, pre, step_raw,
    rows, weights, step_buf, total, step_total,
    weight_sem, step_sem, send_left, send_right, recv_sem,
):
    me = lax.axis_index("tp")
    length, depth = tokens.shape
    deep = depth // quarters
    step_copy = pltpu.make_async_copy(step_w, step_buf, step_sem)
    step_copy.start()
    for q in range(quarters):
        tile = 0
        for source in (gate_w, value_w, key_w, query_w):
            for part in range(source.shape[1] // TILE):
                pltpu.make_async_copy(
                    source.at[pl.ds(q * deep, deep), pl.ds(part * TILE, TILE)],
                    weights.at[q, tile // 2, :, pl.ds(tile % 2 * TILE, TILE)], weight_sem.at[q, tile],
                ).start()
                tile += 1

    def place(chunk):
        return pl.ds(pl.multiple_of(chunk * length, length), length)

    for q in range(quarters):
        rows[q, place(me), :] = tokens[:, q * deep:(q + 1) * deep]
    greet([("tp", me - 1, me > 0), ("tp", me + 1, me < n - 1)])

    def rightward(q, chunk):
        spot = rows.at[q, place(chunk)]
        return pltpu.make_async_remote_copy(
            src_ref=spot, dst_ref=spot,
            send_sem=send_right.at[q, chunk], recv_sem=recv_sem.at[q, chunk],
            device_id={"tp": me + 1}, device_id_type=MESH,
        )

    def leftward(q, chunk):
        spot = rows.at[q, place(chunk)]
        return pltpu.make_async_remote_copy(
            src_ref=spot, dst_ref=spot,
            send_sem=send_left.at[q, chunk], recv_sem=recv_sem.at[q, chunk],
            device_id={"tp": me - 1}, device_id_type=MESH,
        )

    for q in range(quarters):

        @pl.when(me < n - 1)
        def _():
            rightward(q, me).start()

        @pl.when(me > 0)
        def _():
            leftward(q, me).start()

    def receive(q, far):
        below, above = me - far, me + far

        @pl.when(below >= 0)
        def _():
            rightward(q, below).wait_recv()

            @pl.when(me < n - 1)
            def _():
                rightward(q, below).start()

        @pl.when(above < n)
        def _():
            leftward(q, above).wait_recv()

            @pl.when(me > 0)
            def _():
                leftward(q, above).start()

    for far in range(1, n - 1):
        for q in range(quarters):
            receive(q, far)
    step_copy.wait()
    for q in range(quarters):
        receive(q, n - 1)

        def one(pair, _):
            for half in range(2):
                pltpu.make_async_copy(
                    gate_w.at[pl.ds(0, deep), pl.ds(0, TILE)],
                    weights.at[q, pair, :, pl.ds(half * TILE, TILE)], weight_sem.at[q, 2 * pair + half],
                ).wait()
            added = jnp.dot(rows[q], weights[q, pair], preferred_element_type=jnp.float32)
            if q > 0:
                added = total[pair] + added
            if q < quarters - 1:
                total[pair] = added
            else:
                for half in range(2):
                    pre[2 * pair + half] = added[:, half * TILE:(half + 1) * TILE].astype(jnp.bfloat16)
            return 0

        lax.fori_loop(0, tiles // 2, one, 0)
        added = lax.dot_general(
            rows[q], step_buf[:, q * deep:(q + 1) * deep], (((1,), (1,)), ((), ())),
            preferred_element_type=jnp.float32,
        )
        if q > 0:
            added = step_total[...] + added
        if q < quarters - 1:
            step_total[...] = added
        else:
            step_raw[...] = added

    for q in range(quarters):
        for chunk in range(n):

            @pl.when(jnp.logical_and(chunk <= me, me < n - 1))
            def _():
                rightward(q, chunk).wait_send()

            @pl.when(jnp.logical_and(chunk >= me, me > 0))
            def _():
                leftward(q, chunk).wait_send()


def silu(v):
    return v / (1.0 + jnp.exp(-v))


def three_parts(array):
    high = array.astype(jnp.bfloat16)
    rest = array - high.astype(jnp.float32)
    middle = rest.astype(jnp.bfloat16)
    low = (rest - middle.astype(jnp.float32)).astype(jnp.bfloat16)
    return jnp.concatenate([high, middle, low], axis=1)


def layer_kernel(
    n, slabs, value_tiles, key_tiles,
    pre, step_raw, value_conv, key_conv, query_conv, step_bias, decay_log, skip_gain, norm_gain, out_w,
    out,
    border, edge_buf, padded, keys, queries, scores, acts, cum_s, cum_t, step_t, tail_s, grow_s,
    grow_x, local0, slab, leaving, inflow, starts, gated, squares, normed, weight, partial, from_left, from_right,
    edge_send, edge_recv, state_send, state_recv, weight_sem, part_send, left_recv, right_recv,
):
    me = lax.axis_index("tp")
    ctx = lax.axis_index("ctx")
    slab_rows, heads = step_raw.shape
    blocks = slab_rows // BLOCK
    length = slab_rows // n
    kernel_len = value_conv.shape[0]
    conv_tiles = value_tiles + 2 * key_tiles
    group_tiles = INNER // GROUPS // TILE
    width = TILE // (value_tiles * TILE // heads)
    last = slab_rows - 16
    pieces = partial.shape[1]
    piece = partial.shape[3]
    weight_copy = pltpu.make_async_copy(out_w, weight, weight_sem)
    weight_copy.start()
    for t in range(conv_tiles):
        edge_buf[t] = pre[value_tiles + t, pl.ds(last, 16), :]
    greet([
        ("tp", me - 1, me > 0), ("tp", me + 1, me < n - 1),
        ("ctx", ctx - 1, ctx > 0), ("ctx", ctx + 1, ctx < slabs - 1),
    ])
    edge = pltpu.make_async_remote_copy(
        src_ref=edge_buf, dst_ref=border, send_sem=edge_send, recv_sem=edge_recv,
        device_id={"ctx": ctx + 1}, device_id_type=MESH,
    )

    @pl.when(ctx < slabs - 1)
    def _():
        edge.start()

    @pl.when(ctx == 0)
    def _():
        border[...] = jnp.zeros_like(border)
        inflow[...] = jnp.zeros_like(inflow)

    row = lax.broadcasted_iota(jnp.int32, (BLOCK, BLOCK), 0)
    col = lax.broadcasted_iota(jnp.int32, (BLOCK, BLOCK), 1)
    causal = row >= col
    lower = jnp.where(causal, 1.0, 0.0)
    upper = jnp.where(row <= col, 1.0, 0.0)
    same = jnp.where(row == col, 1.0, 0.0)
    turned = (((0,), (0,)), ((), ()))
    raw = step_raw[...] + step_bias[...]
    step = jnp.maximum(raw, 0.0) + jnp.log1p(jnp.exp(-jnp.abs(raw)))
    rate = -jnp.exp(decay_log[...]) * step
    for b in range(blocks):
        lo = b * BLOCK
        rate_b, step_b = rate[lo:lo + BLOCK], step[lo:lo + BLOCK]
        cum = jnp.dot(lower, rate_b, precision=EXACT, preferred_element_type=jnp.float32)
        cum_s[pl.ds(lo, BLOCK), :] = three_parts(cum)
        cum_t[b] = lax.dot_general(rate_b, upper, turned, precision=EXACT, preferred_element_type=jnp.float32)
        step_t[b] = lax.dot_general(step_b, same, turned, precision=EXACT, preferred_element_type=jnp.float32)
        tail_s[pl.ds(lo, BLOCK), :] = three_parts(jnp.exp(cum[BLOCK - 1:BLOCK] - cum) * step_b)
        grow_s[pl.ds(lo, BLOCK), :] = three_parts(jnp.exp(cum))

    def convolve(t, taps):
        padded[pl.ds(0, 16), :] = border[t].astype(jnp.float32)
        padded[pl.ds(16, slab_rows), :] = pre[value_tiles + t].astype(jnp.float32)
        total = padded[pl.ds(17 - kernel_len, slab_rows), :] * taps[0:1]
        for k in range(1, kernel_len):
            total = total + padded[pl.ds(17 - kernel_len + k, slab_rows), :] * taps[k:k + 1]
        return silu(total).astype(jnp.bfloat16)

    @pl.when(ctx > 0)
    def _():
        edge.wait_recv()

    per_tile = TILE // STATE
    for t in range(key_tiles):
        cols = slice(t * TILE, (t + 1) * TILE)
        key = convolve(value_tiles + t, key_conv[:, cols])
        query = convolve(value_tiles + key_tiles + t, query_conv[:, cols])
        for g in range(per_tile):
            keys[t * per_tile + g] = key[:, g * STATE:(g + 1) * STATE]
            queries[t * per_tile + g] = query[:, g * STATE:(g + 1) * STATE]
    for g in range(key_tiles * per_tile):
        for b in range(blocks):
            lo = b * BLOCK
            scores[g, b] = lax.dot_general(
                queries[g, pl.ds(lo, BLOCK), :], keys[g, pl.ds(lo, BLOCK), :],
                (((1,), (1,)), ((), ())), preferred_element_type=jnp.float32,
            )

    def spread(t, each, count):
        head = lax.broadcasted_iota(jnp.int32, (3 * heads, each * count), 0) % heads
        lane = lax.broadcasted_iota(jnp.int32, (3 * heads, each * count), 1)
        return jnp.where(head == t * count + lane // each, 1.0, 0.0).astype(jnp.bfloat16)

    def widen(array, matrix):
        return jnp.dot(array, matrix, preferred_element_type=jnp.float32)

    def state_copy(t):
        return pltpu.make_async_remote_copy(
            src_ref=leaving.at[t], dst_ref=inflow.at[t],
            send_sem=state_send.at[t], recv_sem=state_recv.at[t],
            device_id={"ctx": ctx + 1}, device_id_type=MESH,
        )

    def first_pass(t, _):
        place = pl.ds(pl.multiple_of(t * TILE, TILE), TILE)
        value = convolve(t, value_conv[:, place])
        acts[t] = value
        chooser = spread(t, TILE // width, width)
        tail = widen(tail_s[...], chooser)
        grow = widen(grow_s[...], chooser)
        grow_x[t] = grow
        weighted = (value.astype(jnp.float32) * tail).astype(jnp.bfloat16)
        g = t // group_tiles
        state = jnp.zeros((STATE, TILE), jnp.float32)
        for b in range(blocks):
            lo = b * BLOCK
            added = lax.dot_general(
                keys[g, pl.ds(lo, BLOCK), :], weighted[lo:lo + BLOCK], turned,
                preferred_element_type=jnp.float32,
            )
            state = grow[lo + BLOCK - 1:lo + BLOCK] * state + added
            if b == 0:
                local0[t] = state
        slab[t] = state

        @pl.when(ctx == 0)
        def _():
            leaving[t] = state.astype(jnp.bfloat16)
            if slabs > 1:
                state_copy(t).start()

        return 0

    lax.fori_loop(0, value_tiles, first_pass, 0)
    squares[...] = jnp.zeros_like(squares)
    skip_parts = three_parts(jnp.broadcast_to(skip_gain[...], (16, heads)))
    left_half = lax.broadcasted_iota(jnp.int32, (BLOCK, BLOCK), 1) < TILE // width

    def enter(t):
        grow = grow_x[t]

        @pl.when(ctx > 0)
        def _():
            state_copy(t).wait_recv()

        start = inflow[t].astype(jnp.float32)
        after = grow[BLOCK - 1:BLOCK] * start + local0[t]
        starts[0, t] = inflow[t]
        starts[1, t] = after.astype(jnp.bfloat16)

        @pl.when(jnp.logical_and(ctx > 0, ctx < slabs - 1))
        def _():
            fall = grow[BLOCK - 1:BLOCK] * grow[2 * BLOCK - 1:2 * BLOCK]
            leaving[t] = (fall * start + slab[t]).astype(jnp.bfloat16)
            state_copy(t).start()

    def second_pass(b, first):
        rows_b = pl.ds(pl.multiple_of(b * BLOCK, BLOCK), BLOCK)

        def one(t, _):
            if first:
                enter(t)
            g = t // group_tiles
            columns = widen(cum_s[rows_b, :], spread(t, BLOCK, width))
            skip = widen(skip_parts, spread(t, TILE // width, width))[0:1]
            value = acts[t, rows_b, :]
            score = scores[g, b]
            parts = []
            for pair in range(width // 2):
                both = []
                for k in (2 * pair, 2 * pair + 1):
                    h = t * width + k
                    diff = columns[:, k * BLOCK:(k + 1) * BLOCK] - cum_t[b, pl.ds(h, 1), :]
                    factor = jnp.exp(jnp.where(causal, diff, -1e30))
                    mix = (score * factor * step_t[b, pl.ds(h, 1), :]).astype(jnp.bfloat16)
                    both.append(jnp.dot(
                        mix, value[:, pair * BLOCK:(pair + 1) * BLOCK], preferred_element_type=jnp.float32
                    ))
                parts.append(jnp.where(left_half, both[0], both[1]))
            inner = jnp.concatenate(parts, axis=1)
            outer = jnp.dot(queries[g, rows_b, :], starts[b, t], preferred_element_type=jnp.float32)
            ssm = inner + grow_x[t, rows_b, :] * outer + skip * value.astype(jnp.float32)
            result = ssm * silu(pre[t, rows_b, :].astype(jnp.float32))
            gated[t, rows_b, :] = result
            squares[g, rows_b, :] += result * result
            return 0

        lax.fori_loop(0, value_tiles, one, 0)
        for g in range(value_tiles // group_tiles):
            total = jnp.sum(squares[g, rows_b, :], axis=1, keepdims=True)
            scale = lax.rsqrt(total / (INNER // GROUPS) + 1e-05)
            for t in range(g * group_tiles, (g + 1) * group_tiles):
                cols = slice(t * TILE, (t + 1) * TILE)
                normed[rows_b, cols] = (
                    gated[t, rows_b, :] * scale * norm_gain[:, cols]
                ).astype(jnp.bfloat16)

    def product(b, p):
        rows = normed[pl.ds(pl.multiple_of(b * length, length), length), :]
        return jnp.dot(
            rows, weight[:, pl.ds(pl.multiple_of(p * piece, piece), piece)],
            preferred_element_type=jnp.float32,
        )

    def rightward(b, p):
        return pltpu.make_async_remote_copy(
            src_ref=partial.at[b, p], dst_ref=from_left.at[b, p],
            send_sem=part_send.at[b, p], recv_sem=left_recv.at[b, p],
            device_id={"tp": me + 1}, device_id_type=MESH,
        )

    def leftward(b, p):
        return pltpu.make_async_remote_copy(
            src_ref=partial.at[b, p], dst_ref=from_right.at[b, p],
            send_sem=part_send.at[b, p], recv_sem=right_recv.at[b, p],
            device_id={"tp": me - 1}, device_id_type=MESH,
        )

    def send(far):
        above, below = me + far, me - far

        def forward(p, _):
            @pl.when(above < n)
            def _():
                mine = product(above, p)

                @pl.when(me == 0)
                def _():
                    partial[above, p] = mine.astype(jnp.bfloat16)

                @pl.when(me > 0)
                def _():
                    rightward(above, p).wait_recv()
                    partial[above, p] = (
                        mine + from_left[above, p].astype(jnp.float32)
                    ).astype(jnp.bfloat16)

                rightward(above, p).start()

            @pl.when(below >= 0)
            def _():
                mine = product(below, p)

                @pl.when(me == n - 1)
                def _():
                    partial[below, p] = mine.astype(jnp.bfloat16)

                @pl.when(me < n - 1)
                def _():
                    leftward(below, p).wait_recv()
                    partial[below, p] = (
                        mine + from_right[below, p].astype(jnp.float32)
                    ).astype(jnp.bfloat16)

                leftward(below, p).start()

            return 0

        lax.fori_loop(0, pieces, forward, 0)

    first_block = 1 - me // (n // 2)
    at_end = jnp.logical_or(me == 0, me == n - 1)
    second_pass(first_block, True)
    weight_copy.wait()

    @pl.when(at_end)
    def _():
        for far in range(n - 1, n // 2 - 1, -1):
            send(far)

    second_pass(1 - first_block, False)

    @pl.when(jnp.logical_not(at_end))
    def _():
        for far in range(n - 2, n // 2 - 1, -1):
            send(far)

    for far in range(n // 2 - 1, 0, -1):
        send(far)

    for p in range(pieces):
        cols = pl.ds(p * piece, piece)
        partial[me, p] = product(me, p).astype(jnp.bfloat16)

    @pl.when(me == 0)
    def _():
        from_left[me] = jnp.zeros(from_left.shape[1:], from_left.dtype)

    @pl.when(me == n - 1)
    def _():
        from_right[me] = jnp.zeros(from_right.shape[1:], from_right.dtype)

    for p in range(pieces):
        cols = pl.ds(p * piece, piece)

        @pl.when(me > 0)
        def _():
            rightward(me, p).wait_recv()

        @pl.when(me < n - 1)
        def _():
            leftward(me, p).wait_recv()

        out[:, cols] = (
            partial[me, p].astype(jnp.float32)
            + from_left[me, p].astype(jnp.float32)
            + from_right[me, p].astype(jnp.float32)
        ).astype(out.dtype)

    for b in range(n):

        @pl.when(b != me)
        def _():
            for p in range(pieces):
                rightward(b, p).wait_send()

    @pl.when(ctx < slabs - 1)
    def _():
        edge.wait_send()
        for t in range(value_tiles):
            state_copy(t).wait_send()


def fused(n, slabs, tokens, gate_weight, value_weight, key_weight, query_weight, step_weight,
          value_conv, key_conv, query_conv, step_bias, decay_log, skip_gain, norm_gain, out_weight):
    length, depth = tokens.shape
    if length * n != 2 * BLOCK or n != 4:
        return shards(
            tokens, gate_weight, value_weight, key_weight, query_weight, step_weight, value_conv, key_conv,
            query_conv, step_bias, decay_log, skip_gain, norm_gain, out_weight,
        )
    columns = gate_weight.shape[1]
    key_cols = key_weight.shape[1]
    heads = step_weight.shape[1]
    slab_rows = length * n
    value_tiles, key_tiles = columns // TILE, key_cols // TILE
    tiles = 2 * value_tiles + 2 * key_tiles
    quarters = 4
    deep = depth // quarters
    bf16, f32 = jnp.bfloat16, jnp.float32
    vmem, anywhere = pl.BlockSpec(memory_space=pltpu.VMEM), pl.BlockSpec(memory_space=pl.ANY)
    dma = pltpu.SemaphoreType.DMA
    pre, step_raw = pl.pallas_call(
        functools.partial(project_kernel, n, tiles, quarters),
        out_shape=(
            jax.ShapeDtypeStruct((tiles, slab_rows, TILE), bf16),
            jax.ShapeDtypeStruct((slab_rows, heads), f32),
        ),
        in_specs=[vmem] + [anywhere] * 5,
        out_specs=(vmem, vmem),
        scratch_shapes=[
            pltpu.VMEM((quarters, slab_rows, deep), bf16),
            pltpu.VMEM((quarters, tiles // 2, deep, 2 * TILE), bf16),
            pltpu.VMEM((heads, depth), bf16),
            pltpu.VMEM((tiles // 2, slab_rows, 2 * TILE), f32),
            pltpu.VMEM((slab_rows, heads), f32),
            dma((quarters, tiles)), dma, dma((quarters, n)), dma((quarters, n)), dma((quarters, n)),
        ],
        compiler_params=pltpu.CompilerParams(
            collective_id=0, has_side_effects=True, vmem_limit_bytes=56 * 2**20
        ),
    )(tokens, gate_weight, value_weight, key_weight, query_weight, step_weight.T)
    blocks = slab_rows // BLOCK
    groups_here = key_cols // STATE
    out_cols = out_weight.shape[1]
    piece = 1024
    pieces = out_cols // piece
    wide = (value_tiles, slab_rows, TILE)
    conv_tiles = value_tiles + 2 * key_tiles
    return pl.pallas_call(
        functools.partial(layer_kernel, n, slabs, value_tiles, key_tiles),
        out_shape=jax.ShapeDtypeStruct((length, out_cols), bf16),
        in_specs=[vmem] * 9 + [anywhere],
        out_specs=vmem,
        scratch_shapes=[
            pltpu.VMEM((conv_tiles, 16, TILE), bf16),
            pltpu.VMEM((conv_tiles, 16, TILE), bf16),
            pltpu.VMEM((slab_rows + 16, TILE), f32),
            pltpu.VMEM((groups_here, slab_rows, STATE), bf16),
            pltpu.VMEM((groups_here, slab_rows, STATE), bf16),
            pltpu.VMEM((groups_here, blocks, BLOCK, BLOCK), f32),
            pltpu.VMEM(wide, bf16),
            pltpu.VMEM((slab_rows, 3 * heads), bf16),
            pltpu.VMEM((blocks, heads, BLOCK), f32),
            pltpu.VMEM((blocks, heads, BLOCK), f32),
            pltpu.VMEM((slab_rows, 3 * heads), bf16),
            pltpu.VMEM((slab_rows, 3 * heads), bf16),
            pltpu.VMEM(wide, f32),
            pltpu.VMEM((value_tiles, STATE, TILE), f32),
            pltpu.VMEM((value_tiles, STATE, TILE), f32),
            pltpu.VMEM((value_tiles, STATE, TILE), bf16),
            pltpu.VMEM((value_tiles, STATE, TILE), bf16),
            pltpu.VMEM((2, value_tiles, STATE, TILE), bf16),
            pltpu.VMEM(wide, f32),
            pltpu.VMEM((groups_here, slab_rows, TILE), f32),
            pltpu.VMEM((slab_rows, columns), bf16),
            pltpu.VMEM(out_weight.shape, bf16),
            pltpu.VMEM((n, pieces, length, piece), bf16),
            pltpu.VMEM((n, pieces, length, piece), bf16),
            pltpu.VMEM((n, pieces, length, piece), bf16),
            dma, dma, dma((value_tiles,)), dma((value_tiles,)), dma,
            dma((n, pieces)), dma((n, pieces)), dma((n, pieces)),
        ],
        compiler_params=pltpu.CompilerParams(
            collective_id=1, has_side_effects=True, vmem_limit_bytes=56 * 2**20
        ),
    )(
        pre, step_raw, value_conv, key_conv, query_conv, step_bias[None], decay_log[None],
        skip_gain[None], norm_gain[None], out_weight,
    )


def solution(mesh):
    n, slabs = mesh.shape["tp"], mesh.shape["ctx"]
    whole_groups = INNER // n % (INNER // GROUPS) == 0 and GROUPS * STATE // n % TILE == 0
    body = functools.partial(fused, n, slabs) if whole_groups and n >= 4 else shards
    return jax.shard_map(
        body,
        mesh=mesh,
        in_specs=(
            P(("groups", "ctx", "tp"), None),
            P(None, "tp"),
            P(None, "tp"),
            P(None, "tp"),
            P(None, "tp"),
            P(None, "tp"),
            P(None, "tp"),
            P(None, "tp"),
            P(None, "tp"),
            P("tp"),
            P("tp"),
            P("tp"),
            P("tp"),
            P("tp", None),
        ),
        out_specs=P(("groups", "ctx", "tp"), None),
        check_vma=False,
    )
```

```python
import functools

import jax
import jax.numpy as jnp
from jax import lax
from jax.experimental import pallas as pl
from jax.experimental.pallas import tpu as pltpu
from jax.sharding import PartitionSpec as P

STATE = 128
GROUPS = 8
INNER = 8192


def passed_along(shard, axis, by):
    count = lax.axis_size(axis)
    pairs = [(i, i + by) for i in range(count) if 0 <= i + by < count]
    return lax.ppermute(shard, axis, pairs)


def from_partner(block, axis, distance):
    count = lax.axis_size(axis)
    route = []
    for low in range(count):
        high = low | 1 << distance
        if high != low and high < count:
            route += [(low, high), (high, low)]
    return lax.ppermute(block, axis, route)


def causal_mix(padded, kernel, length):
    total = padded[0:length] * kernel[0]
    for tap_index in range(1, kernel.shape[0]):
        total = total + padded[tap_index : tap_index + length] * kernel[tap_index]
    return total


def shards(
    tokens,
    gate_weight,
    value_weight,
    key_weight,
    query_weight,
    step_weight,
    value_conv,
    key_conv,
    query_conv,
    step_bias,
    decay_log,
    skip_gain,
    norm_gain,
    out_weight,
):
    tok_dev = tokens.shape[0]
    slab_rows = tok_dev * lax.axis_size("tp")
    columns = gate_weight.shape[1]
    key_cols = key_weight.shape[1]
    heads_here = step_weight.shape[1]
    head_width = columns // heads_here
    block_len = min(128, slab_rows)
    block_count = slab_rows // block_len
    kernel_len = value_conv.shape[0]
    joined = jnp.concatenate(
        [gate_weight, value_weight, key_weight, query_weight, step_weight], axis=1
    )
    projected = jnp.dot(
        lax.all_gather(tokens, "tp", axis=0, tiled=True), joined, preferred_element_type=jnp.float32
    )
    gate_in = projected[:, :columns].astype(jnp.bfloat16)
    mixed_pre = projected[:, columns : 2 * columns + 2 * key_cols].astype(jnp.bfloat16)
    step_raw = projected[:, 2 * columns + 2 * key_cols :]
    border = passed_along(mixed_pre[slab_rows - (kernel_len - 1) :], "ctx", 1)
    padded = jnp.concatenate([border, mixed_pre], axis=0).astype(jnp.float32)
    kernel = jnp.concatenate([value_conv, key_conv, query_conv], axis=1)
    activated = jax.nn.silu(causal_mix(padded, kernel, slab_rows)).astype(jnp.bfloat16)
    value_act = activated[:, :columns]
    key_act = activated[:, columns : columns + key_cols]
    query_act = activated[:, columns + key_cols :]
    group_cols = max(key_cols, STATE)
    reach = group_cols // key_cols
    key_group, query_group = (key_act, query_act)
    for bit_index in range(reach.bit_length() - 1):
        other_keys, other_queries = from_partner((key_group, query_group), "tp", bit_index)
        upper = lax.axis_index("tp") // (1 << bit_index) % 2 == 1
        key_group = jnp.where(
            upper,
            jnp.concatenate([other_keys, key_group], 1),
            jnp.concatenate([key_group, other_keys], 1),
        )
        query_group = jnp.where(
            upper,
            jnp.concatenate([other_queries, query_group], 1),
            jnp.concatenate([query_group, other_queries], 1),
        )
    local_groups = group_cols // STATE
    per_group = heads_here // local_groups
    step = jax.nn.softplus(step_raw + step_bias)
    rate = -jnp.exp(decay_log) * step
    cum = jnp.cumsum(rate.reshape(block_count, block_len, heads_here), axis=1)
    step_blk = step.reshape(block_count, block_len, heads_here)
    values = value_act.reshape(block_count, block_len, heads_here, head_width)
    keys = key_group.reshape(block_count, block_len, local_groups, STATE)
    queries = query_group.reshape(block_count, block_len, local_groups, STATE)
    scores = jnp.einsum("btgn,bugn->gbtu", queries, keys, preferred_element_type=jnp.float32)
    scores = jnp.repeat(scores, per_group, axis=0)
    cum_t = jnp.transpose(cum, (2, 0, 1))
    step_t = jnp.transpose(step_blk, (2, 0, 1))
    causal = jnp.tril(jnp.ones((block_len, block_len), jnp.bool_))
    diff = cum_t[:, :, :, None] - cum_t[:, :, None, :]
    factor = jnp.where(causal, jnp.exp(jnp.where(causal, diff, 0.0)), 0.0)
    weights = (scores * factor * step_t[:, :, None, :]).astype(jnp.bfloat16)
    inner = jnp.einsum("hbtu,buhp->bthp", weights, values, preferred_element_type=jnp.float32)
    tail = jnp.exp(cum[:, -1:, :] - cum) * step_blk
    weighted = (values * tail[:, :, :, None]).astype(jnp.bfloat16)
    key_heads = jnp.repeat(keys, per_group, axis=2)
    query_heads = jnp.repeat(queries, per_group, axis=2)
    local = jnp.einsum("buhn,buhp->bhnp", key_heads, weighted, preferred_element_type=jnp.float32)
    falloff = jnp.exp(cum[:, -1, :])

    def advance(carry, item):
        fade, added = item
        return (fade[:, None, None] * carry + added, carry)

    zero_state = jnp.zeros((heads_here, STATE, head_width), jnp.float32)
    slab_state, _ = lax.scan(advance, zero_state, (falloff, local))
    slab_fall = jnp.exp(jnp.sum(cum[:, -1, :], axis=0))
    inflow = zero_state
    for turn in range(lax.axis_size("ctx") - 1):
        inflow = passed_along(
            (slab_fall[:, None, None] * inflow + slab_state).astype(jnp.bfloat16), "ctx", 1
        ).astype(jnp.float32)
    _, starts = lax.scan(advance, inflow, (falloff, local))
    outer = jnp.einsum(
        "bthn,bhnp->bthp", query_heads.astype(jnp.float32), starts, precision=lax.Precision.HIGHEST
    )
    ssm_out = (
        inner
        + jnp.exp(cum)[:, :, :, None] * outer
        + skip_gain[:, None] * values.astype(jnp.float32)
    )
    ssm_out = ssm_out.reshape(slab_rows, columns)
    gated = ssm_out * jax.nn.silu(gate_in.astype(jnp.float32))
    span = INNER // GROUPS
    piece_len = min(columns, span)
    norm_here = columns // piece_len
    squares = jnp.sum((gated * gated).reshape(slab_rows, norm_here, piece_len), axis=2)
    norm_reach = span // piece_len
    for bit_index in range(norm_reach.bit_length() - 1):
        squares = squares + from_partner(squares, "tp", bit_index)
    scale = lax.rsqrt(squares / span + 1e-05)
    normed = (gated.reshape(slab_rows, norm_here, piece_len) * scale[:, :, None]).reshape(
        slab_rows, columns
    ) * norm_gain
    normed = normed.astype(jnp.bfloat16)
    return lax.psum_scatter(
        jnp.dot(normed, out_weight, preferred_element_type=jnp.float32).astype(jnp.bfloat16),
        "tp",
        scatter_dimension=0,
        tiled=True,
    )


TILE = 256
BLOCK = 128
MESH = pl.DeviceIdType.MESH
EXACT = lax.Precision.HIGHEST


def greet(neighbours):
    barrier = pltpu.get_barrier_semaphore()
    count = 0
    for axis, index, exists in neighbours:

        @pl.when(exists)
        def _():
            pl.semaphore_signal(barrier, inc=1, device_id={axis: index}, device_id_type=MESH)

        count = count + exists.astype(jnp.int32)
    pl.semaphore_wait(barrier, count)


def project_kernel(
    n, tiles, quarters, tokens, gate_w, value_w, key_w, query_w, step_w, pre, step_raw,
    rows, weights, step_buf, total, step_total,
    weight_sem, step_sem, send_left, send_right, recv_sem,
):
    me = lax.axis_index("tp")
    length, depth = tokens.shape
    deep = depth // quarters
    step_copy = pltpu.make_async_copy(step_w, step_buf, step_sem)
    step_copy.start()
    for q in range(quarters):
        tile = 0
        for source in (gate_w, value_w, key_w, query_w):
            for part in range(source.shape[1] // TILE):
                pltpu.make_async_copy(
                    source.at[pl.ds(q * deep, deep), pl.ds(part * TILE, TILE)],
                    weights.at[q, tile // 2, :, pl.ds(tile % 2 * TILE, TILE)], weight_sem.at[q, tile],
                ).start()
                tile += 1

    def place(chunk):
        return pl.ds(pl.multiple_of(chunk * length, length), length)

    for q in range(quarters):
        rows[q, place(me), :] = tokens[:, q * deep:(q + 1) * deep]
    greet([("tp", me - 1, me > 0), ("tp", me + 1, me < n - 1)])

    def rightward(q, chunk):
        spot = rows.at[q, place(chunk)]
        return pltpu.make_async_remote_copy(
            src_ref=spot, dst_ref=spot,
            send_sem=send_right.at[q, chunk], recv_sem=recv_sem.at[q, chunk],
            device_id={"tp": me + 1}, device_id_type=MESH,
        )

    def leftward(q, chunk):
        spot = rows.at[q, place(chunk)]
        return pltpu.make_async_remote_copy(
            src_ref=spot, dst_ref=spot,
            send_sem=send_left.at[q, chunk], recv_sem=recv_sem.at[q, chunk],
            device_id={"tp": me - 1}, device_id_type=MESH,
        )

    for q in range(quarters):

        @pl.when(me < n - 1)
        def _():
            rightward(q, me).start()

        @pl.when(me > 0)
        def _():
            leftward(q, me).start()

    def receive(q, far):
        below, above = me - far, me + far

        @pl.when(below >= 0)
        def _():
            rightward(q, below).wait_recv()

            @pl.when(me < n - 1)
            def _():
                rightward(q, below).start()

        @pl.when(above < n)
        def _():
            leftward(q, above).wait_recv()

            @pl.when(me > 0)
            def _():
                leftward(q, above).start()

    def multiply(q, half, first):
        part = pl.ds(pl.multiple_of(half * 2 * length, 2 * length), 2 * length)

        def one(pair, _):
            if first:
                for side in range(2):
                    pltpu.make_async_copy(
                        gate_w.at[pl.ds(0, deep), pl.ds(0, TILE)],
                        weights.at[q, pair, :, pl.ds(side * TILE, TILE)], weight_sem.at[q, 2 * pair + side],
                    ).wait()
            added = jnp.dot(rows[q, part, :], weights[q, pair], preferred_element_type=jnp.float32)
            if q > 0:
                added = total[pair, part, :] + added
            if q < quarters - 1:
                total[pair, part, :] = added
            else:
                for side in range(2):
                    pre[2 * pair + side, part, :] = added[:, side * TILE:(side + 1) * TILE].astype(jnp.bfloat16)
            return 0

        lax.fori_loop(0, tiles // 2, one, 0)
        added = lax.dot_general(
            rows[q, part, :], step_buf[:, q * deep:(q + 1) * deep], (((1,), (1,)), ((), ())),
            preferred_element_type=jnp.float32,
        )
        if q > 0:
            added = step_total[part, :] + added
        if q < quarters - 1:
            step_total[part, :] = added
        else:
            step_raw[part, :] = added

    own = me // 2
    step_copy.wait()
    for q in range(quarters):
        receive(q, 1)
        multiply(q, own, True)
    for q in range(quarters):
        receive(q, 2)
    for q in range(quarters):
        receive(q, 3)
        multiply(q, 1 - own, False)

    for q in range(quarters):
        for chunk in range(n):

            @pl.when(jnp.logical_and(chunk <= me, me < n - 1))
            def _():
                rightward(q, chunk).wait_send()

            @pl.when(jnp.logical_and(chunk >= me, me > 0))
            def _():
                leftward(q, chunk).wait_send()


def silu(v):
    return v / (1.0 + jnp.exp(-v))


def three_parts(array):
    high = array.astype(jnp.bfloat16)
    rest = array - high.astype(jnp.float32)
    middle = rest.astype(jnp.bfloat16)
    low = (rest - middle.astype(jnp.float32)).astype(jnp.bfloat16)
    return jnp.concatenate([high, middle, low], axis=1)


def layer_kernel(
    n, slabs, value_tiles, key_tiles,
    pre, step_raw, value_conv, key_conv, query_conv, step_bias, decay_log, skip_gain, norm_gain, out_w,
    out,
    border, edge_buf, padded, keys, queries, scores, acts, cum_s, cum_t, step_t, tail_s, grow_s,
    grow_x, local0, slab, leaving, inflow, starts, gated, squares, normed, weight, partial, from_left, from_right,
    edge_send, edge_recv, state_send, state_recv, weight_sem, part_send, left_recv, right_recv,
):
    me = lax.axis_index("tp")
    ctx = lax.axis_index("ctx")
    slab_rows, heads = step_raw.shape
    blocks = slab_rows // BLOCK
    length = slab_rows // n
    kernel_len = value_conv.shape[0]
    conv_tiles = value_tiles + 2 * key_tiles
    group_tiles = INNER // GROUPS // TILE
    width = TILE // (value_tiles * TILE // heads)
    last = slab_rows - 16
    pieces = partial.shape[1]
    piece = partial.shape[3]
    weight_copy = pltpu.make_async_copy(out_w, weight, weight_sem)
    weight_copy.start()
    for t in range(conv_tiles):
        edge_buf[t] = pre[value_tiles + t, pl.ds(last, 16), :]
    greet([
        ("tp", me - 1, me > 0), ("tp", me + 1, me < n - 1),
        ("ctx", ctx - 1, ctx > 0), ("ctx", ctx + 1, ctx < slabs - 1),
    ])
    edge = pltpu.make_async_remote_copy(
        src_ref=edge_buf, dst_ref=border, send_sem=edge_send, recv_sem=edge_recv,
        device_id={"ctx": ctx + 1}, device_id_type=MESH,
    )

    @pl.when(ctx < slabs - 1)
    def _():
        edge.start()

    @pl.when(ctx == 0)
    def _():
        border[...] = jnp.zeros_like(border)
        inflow[...] = jnp.zeros_like(inflow)

    row = lax.broadcasted_iota(jnp.int32, (BLOCK, BLOCK), 0)
    col = lax.broadcasted_iota(jnp.int32, (BLOCK, BLOCK), 1)
    causal = row >= col
    lower = jnp.where(causal, 1.0, 0.0)
    upper = jnp.where(row <= col, 1.0, 0.0)
    same = jnp.where(row == col, 1.0, 0.0)
    turned = (((0,), (0,)), ((), ()))
    raw = step_raw[...] + step_bias[...]
    step = jnp.maximum(raw, 0.0) + jnp.log1p(jnp.exp(-jnp.abs(raw)))
    rate = -jnp.exp(decay_log[...]) * step
    for b in range(blocks):
        lo = b * BLOCK
        rate_b, step_b = rate[lo:lo + BLOCK], step[lo:lo + BLOCK]
        cum = jnp.dot(lower, rate_b, precision=EXACT, preferred_element_type=jnp.float32)
        cum_s[pl.ds(lo, BLOCK), :] = three_parts(cum)
        cum_t[b] = lax.dot_general(rate_b, upper, turned, precision=EXACT, preferred_element_type=jnp.float32)
        step_t[b] = lax.dot_general(step_b, same, turned, precision=EXACT, preferred_element_type=jnp.float32)
        tail_s[pl.ds(lo, BLOCK), :] = three_parts(jnp.exp(cum[BLOCK - 1:BLOCK] - cum) * step_b)
        grow_s[pl.ds(lo, BLOCK), :] = three_parts(jnp.exp(cum))

    def convolve(t, taps):
        padded[pl.ds(0, 16), :] = border[t].astype(jnp.float32)
        padded[pl.ds(16, slab_rows), :] = pre[value_tiles + t].astype(jnp.float32)
        total = padded[pl.ds(17 - kernel_len, slab_rows), :] * taps[0:1]
        for k in range(1, kernel_len):
            total = total + padded[pl.ds(17 - kernel_len + k, slab_rows), :] * taps[k:k + 1]
        return silu(total).astype(jnp.bfloat16)

    @pl.when(ctx > 0)
    def _():
        edge.wait_recv()

    per_tile = TILE // STATE
    for t in range(key_tiles):
        cols = slice(t * TILE, (t + 1) * TILE)
        key = convolve(value_tiles + t, key_conv[:, cols])
        query = convolve(value_tiles + key_tiles + t, query_conv[:, cols])
        for g in range(per_tile):
            keys[t * per_tile + g] = key[:, g * STATE:(g + 1) * STATE]
            queries[t * per_tile + g] = query[:, g * STATE:(g + 1) * STATE]
    for g in range(key_tiles * per_tile):
        for b in range(blocks):
            lo = b * BLOCK
            scores[g, b] = lax.dot_general(
                queries[g, pl.ds(lo, BLOCK), :], keys[g, pl.ds(lo, BLOCK), :],
                (((1,), (1,)), ((), ())), preferred_element_type=jnp.float32,
            )

    def spread(t, each, count):
        head = lax.broadcasted_iota(jnp.int32, (3 * heads, each * count), 0) % heads
        lane = lax.broadcasted_iota(jnp.int32, (3 * heads, each * count), 1)
        return jnp.where(head == t * count + lane // each, 1.0, 0.0).astype(jnp.bfloat16)

    def widen(array, matrix):
        return jnp.dot(array, matrix, preferred_element_type=jnp.float32)

    def state_copy(t):
        return pltpu.make_async_remote_copy(
            src_ref=leaving.at[t], dst_ref=inflow.at[t],
            send_sem=state_send.at[t], recv_sem=state_recv.at[t],
            device_id={"ctx": ctx + 1}, device_id_type=MESH,
        )

    def first_pass(t, _):
        place = pl.ds(pl.multiple_of(t * TILE, TILE), TILE)
        value = convolve(t, value_conv[:, place])
        acts[t] = value
        chooser = spread(t, TILE // width, width)
        tail = widen(tail_s[...], chooser)
        grow = widen(grow_s[...], chooser)
        grow_x[t] = grow
        weighted = (value.astype(jnp.float32) * tail).astype(jnp.bfloat16)
        g = t // group_tiles
        state = jnp.zeros((STATE, TILE), jnp.float32)
        for b in range(blocks):
            lo = b * BLOCK
            added = lax.dot_general(
                keys[g, pl.ds(lo, BLOCK), :], weighted[lo:lo + BLOCK], turned,
                preferred_element_type=jnp.float32,
            )
            state = grow[lo + BLOCK - 1:lo + BLOCK] * state + added
            if b == 0:
                local0[t] = state
        slab[t] = state

        @pl.when(ctx == 0)
        def _():
            leaving[t] = state.astype(jnp.bfloat16)
            if slabs > 1:
                state_copy(t).start()

        return 0

    lax.fori_loop(0, value_tiles, first_pass, 0)
    squares[...] = jnp.zeros_like(squares)
    skip_parts = three_parts(jnp.broadcast_to(skip_gain[...], (16, heads)))
    left_half = lax.broadcasted_iota(jnp.int32, (BLOCK, BLOCK), 1) < TILE // width

    def enter(t):
        grow = grow_x[t]

        @pl.when(ctx > 0)
        def _():
            state_copy(t).wait_recv()

        start = inflow[t].astype(jnp.float32)
        after = grow[BLOCK - 1:BLOCK] * start + local0[t]
        starts[0, t] = inflow[t]
        starts[1, t] = after.astype(jnp.bfloat16)

        @pl.when(jnp.logical_and(ctx > 0, ctx < slabs - 1))
        def _():
            fall = grow[BLOCK - 1:BLOCK] * grow[2 * BLOCK - 1:2 * BLOCK]
            leaving[t] = (fall * start + slab[t]).astype(jnp.bfloat16)
            state_copy(t).start()

    def second_pass(b, first):
        rows_b = pl.ds(pl.multiple_of(b * BLOCK, BLOCK), BLOCK)

        def one(t, _):
            if first:
                enter(t)
            g = t // group_tiles
            columns = widen(cum_s[rows_b, :], spread(t, BLOCK, width))
            skip = widen(skip_parts, spread(t, TILE // width, width))[0:1]
            value = acts[t, rows_b, :]
            score = scores[g, b]
            parts = []
            for pair in range(width // 2):
                both = []
                for k in (2 * pair, 2 * pair + 1):
                    h = t * width + k
                    diff = columns[:, k * BLOCK:(k + 1) * BLOCK] - cum_t[b, pl.ds(h, 1), :]
                    factor = jnp.exp(jnp.where(causal, diff, -1e30))
                    mix = (score * factor * step_t[b, pl.ds(h, 1), :]).astype(jnp.bfloat16)
                    both.append(jnp.dot(
                        mix, value[:, pair * BLOCK:(pair + 1) * BLOCK], preferred_element_type=jnp.float32
                    ))
                parts.append(jnp.where(left_half, both[0], both[1]))
            inner = jnp.concatenate(parts, axis=1)
            outer = jnp.dot(queries[g, rows_b, :], starts[b, t], preferred_element_type=jnp.float32)
            ssm = inner + grow_x[t, rows_b, :] * outer + skip * value.astype(jnp.float32)
            result = ssm * silu(pre[t, rows_b, :].astype(jnp.float32))
            gated[t, rows_b, :] = result
            squares[g, rows_b, :] += result * result
            return 0

        lax.fori_loop(0, value_tiles, one, 0)
        for g in range(value_tiles // group_tiles):
            total = jnp.sum(squares[g, rows_b, :], axis=1, keepdims=True)
            scale = lax.rsqrt(total / (INNER // GROUPS) + 1e-05)
            for t in range(g * group_tiles, (g + 1) * group_tiles):
                cols = slice(t * TILE, (t + 1) * TILE)
                normed[rows_b, cols] = (
                    gated[t, rows_b, :] * scale * norm_gain[:, cols]
                ).astype(jnp.bfloat16)

    def product(b, p):
        rows = normed[pl.ds(pl.multiple_of(b * length, length), length), :]
        return jnp.dot(
            rows, weight[:, pl.ds(pl.multiple_of(p * piece, piece), piece)],
            preferred_element_type=jnp.float32,
        )

    def rightward(b, p):
        return pltpu.make_async_remote_copy(
            src_ref=partial.at[b, p], dst_ref=from_left.at[b, p],
            send_sem=part_send.at[b, p], recv_sem=left_recv.at[b, p],
            device_id={"tp": me + 1}, device_id_type=MESH,
        )

    def leftward(b, p):
        return pltpu.make_async_remote_copy(
            src_ref=partial.at[b, p], dst_ref=from_right.at[b, p],
            send_sem=part_send.at[b, p], recv_sem=right_recv.at[b, p],
            device_id={"tp": me - 1}, device_id_type=MESH,
        )

    def send(far):
        above, below = me + far, me - far

        def forward(p, _):
            @pl.when(above < n)
            def _():
                mine = product(above, p)

                @pl.when(me == 0)
                def _():
                    partial[above, p] = mine.astype(jnp.bfloat16)

                @pl.when(me > 0)
                def _():
                    rightward(above, p).wait_recv()
                    partial[above, p] = (
                        mine + from_left[above, p].astype(jnp.float32)
                    ).astype(jnp.bfloat16)

                rightward(above, p).start()

            @pl.when(below >= 0)
            def _():
                mine = product(below, p)

                @pl.when(me == n - 1)
                def _():
                    partial[below, p] = mine.astype(jnp.bfloat16)

                @pl.when(me < n - 1)
                def _():
                    leftward(below, p).wait_recv()
                    partial[below, p] = (
                        mine + from_right[below, p].astype(jnp.float32)
                    ).astype(jnp.bfloat16)

                leftward(below, p).start()

            return 0

        lax.fori_loop(0, pieces, forward, 0)

    first_block = 1 - me // (n // 2)
    at_end = jnp.logical_or(me == 0, me == n - 1)
    second_pass(first_block, True)
    weight_copy.wait()

    @pl.when(at_end)
    def _():
        for far in range(n - 1, n // 2 - 1, -1):
            send(far)

    second_pass(1 - first_block, False)

    @pl.when(jnp.logical_not(at_end))
    def _():
        for far in range(n - 2, n // 2 - 1, -1):
            send(far)

    for far in range(n // 2 - 1, 0, -1):
        send(far)

    for p in range(pieces):
        cols = pl.ds(p * piece, piece)
        partial[me, p] = product(me, p).astype(jnp.bfloat16)

    @pl.when(me == 0)
    def _():
        from_left[me] = jnp.zeros(from_left.shape[1:], from_left.dtype)

    @pl.when(me == n - 1)
    def _():
        from_right[me] = jnp.zeros(from_right.shape[1:], from_right.dtype)

    for p in range(pieces):
        cols = pl.ds(p * piece, piece)

        @pl.when(me > 0)
        def _():
            rightward(me, p).wait_recv()

        @pl.when(me < n - 1)
        def _():
            leftward(me, p).wait_recv()

        out[:, cols] = (
            partial[me, p].astype(jnp.float32)
            + from_left[me, p].astype(jnp.float32)
            + from_right[me, p].astype(jnp.float32)
        ).astype(out.dtype)

    for b in range(n):

        @pl.when(b != me)
        def _():
            for p in range(pieces):
                rightward(b, p).wait_send()

    @pl.when(ctx < slabs - 1)
    def _():
        edge.wait_send()
        for t in range(value_tiles):
            state_copy(t).wait_send()


def fused(n, slabs, tokens, gate_weight, value_weight, key_weight, query_weight, step_weight,
          value_conv, key_conv, query_conv, step_bias, decay_log, skip_gain, norm_gain, out_weight):
    length, depth = tokens.shape
    if length * n != 2 * BLOCK or n != 4:
        return shards(
            tokens, gate_weight, value_weight, key_weight, query_weight, step_weight, value_conv, key_conv,
            query_conv, step_bias, decay_log, skip_gain, norm_gain, out_weight,
        )
    columns = gate_weight.shape[1]
    key_cols = key_weight.shape[1]
    heads = step_weight.shape[1]
    slab_rows = length * n
    value_tiles, key_tiles = columns // TILE, key_cols // TILE
    tiles = 2 * value_tiles + 2 * key_tiles
    quarters = 4
    deep = depth // quarters
    bf16, f32 = jnp.bfloat16, jnp.float32
    vmem, anywhere = pl.BlockSpec(memory_space=pltpu.VMEM), pl.BlockSpec(memory_space=pl.ANY)
    dma = pltpu.SemaphoreType.DMA
    pre, step_raw = pl.pallas_call(
        functools.partial(project_kernel, n, tiles, quarters),
        out_shape=(
            jax.ShapeDtypeStruct((tiles, slab_rows, TILE), bf16),
            jax.ShapeDtypeStruct((slab_rows, heads), f32),
        ),
        in_specs=[vmem] + [anywhere] * 5,
        out_specs=(vmem, vmem),
        scratch_shapes=[
            pltpu.VMEM((quarters, slab_rows, deep), bf16),
            pltpu.VMEM((quarters, tiles // 2, deep, 2 * TILE), bf16),
            pltpu.VMEM((heads, depth), bf16),
            pltpu.VMEM((tiles // 2, slab_rows, 2 * TILE), f32),
            pltpu.VMEM((slab_rows, heads), f32),
            dma((quarters, tiles)), dma, dma((quarters, n)), dma((quarters, n)), dma((quarters, n)),
        ],
        compiler_params=pltpu.CompilerParams(
            collective_id=0, has_side_effects=True, vmem_limit_bytes=56 * 2**20
        ),
    )(tokens, gate_weight, value_weight, key_weight, query_weight, step_weight.T)
    blocks = slab_rows // BLOCK
    groups_here = key_cols // STATE
    out_cols = out_weight.shape[1]
    piece = 1024
    pieces = out_cols // piece
    wide = (value_tiles, slab_rows, TILE)
    conv_tiles = value_tiles + 2 * key_tiles
    return pl.pallas_call(
        functools.partial(layer_kernel, n, slabs, value_tiles, key_tiles),
        out_shape=jax.ShapeDtypeStruct((length, out_cols), bf16),
        in_specs=[vmem] * 9 + [anywhere],
        out_specs=vmem,
        scratch_shapes=[
            pltpu.VMEM((conv_tiles, 16, TILE), bf16),
            pltpu.VMEM((conv_tiles, 16, TILE), bf16),
            pltpu.VMEM((slab_rows + 16, TILE), f32),
            pltpu.VMEM((groups_here, slab_rows, STATE), bf16),
            pltpu.VMEM((groups_here, slab_rows, STATE), bf16),
            pltpu.VMEM((groups_here, blocks, BLOCK, BLOCK), f32),
            pltpu.VMEM(wide, bf16),
            pltpu.VMEM((slab_rows, 3 * heads), bf16),
            pltpu.VMEM((blocks, heads, BLOCK), f32),
            pltpu.VMEM((blocks, heads, BLOCK), f32),
            pltpu.VMEM((slab_rows, 3 * heads), bf16),
            pltpu.VMEM((slab_rows, 3 * heads), bf16),
            pltpu.VMEM(wide, f32),
            pltpu.VMEM((value_tiles, STATE, TILE), f32),
            pltpu.VMEM((value_tiles, STATE, TILE), f32),
            pltpu.VMEM((value_tiles, STATE, TILE), bf16),
            pltpu.VMEM((value_tiles, STATE, TILE), bf16),
            pltpu.VMEM((2, value_tiles, STATE, TILE), bf16),
            pltpu.VMEM(wide, f32),
            pltpu.VMEM((groups_here, slab_rows, TILE), f32),
            pltpu.VMEM((slab_rows, columns), bf16),
            pltpu.VMEM(out_weight.shape, bf16),
            pltpu.VMEM((n, pieces, length, piece), bf16),
            pltpu.VMEM((n, pieces, length, piece), bf16),
            pltpu.VMEM((n, pieces, length, piece), bf16),
            dma, dma, dma((value_tiles,)), dma((value_tiles,)), dma,
            dma((n, pieces)), dma((n, pieces)), dma((n, pieces)),
        ],
        compiler_params=pltpu.CompilerParams(
            collective_id=1, has_side_effects=True, vmem_limit_bytes=56 * 2**20
        ),
    )(
        pre, step_raw, value_conv, key_conv, query_conv, step_bias[None], decay_log[None],
        skip_gain[None], norm_gain[None], out_weight,
    )


def solution(mesh):
    n, slabs = mesh.shape["tp"], mesh.shape["ctx"]
    whole_groups = INNER // n % (INNER // GROUPS) == 0 and GROUPS * STATE // n % TILE == 0
    body = functools.partial(fused, n, slabs) if whole_groups and n >= 4 else shards
    return jax.shard_map(
        body,
        mesh=mesh,
        in_specs=(
            P(("groups", "ctx", "tp"), None),
            P(None, "tp"),
            P(None, "tp"),
            P(None, "tp"),
            P(None, "tp"),
            P(None, "tp"),
            P(None, "tp"),
            P(None, "tp"),
            P(None, "tp"),
            P("tp"),
            P("tp"),
            P("tp"),
            P("tp"),
            P("tp", None),
        ),
        out_specs=P(("groups", "ctx", "tp"), None),
        check_vma=False,
    )
```
